128 devices in a mesh: shot: 4 (over y_lo, core), sub: 32 (over x, y_hi, z).
Axes of the slice: x: 4, y: 4 (y_hi: 2, y_lo: 2; y = y_hi * 2 + y_lo), z: 4, core: 2. Of those that a mesh axis runs over, the one named last changes fastest.
Arguments:
- velocity: float32 [512, 256, 256], P('sub'), may hold values from 1.5 to 4.5
- adjoint_now: float32 [4, 512, 256, 256], P('shot', 'sub'), may hold values from -1.5 to 1.5
- adjoint_prev: float32 [4, 512, 256, 256], P('shot', 'sub'), may hold values from -1.5 to 1.5
- forward_accel: bfloat16 [4, 4, 512, 256, 256], P('shot', None, 'sub'), may hold values from -6 to 6
- traces: float32 [4, 4, 32768], P('shot', None, 'sub'), may hold values from -120 to 120
- receiver_sub: int32 [4, 32768, 1], P('shot', 'sub'), may hold values from 0 to 31; in each aligned block of 1024 rows (0 to 1023, 1024 to 2047, ..., all dimensions but the last counted through in order) at most 64 rows name the same one
- receiver_cell: int32 [4, 32768], P('shot', 'sub'), may hold values from 0 to 1048575
Outputs:
- adjoint_out: float32 [4, 512, 256, 256], P('shot', 'sub')
- gradient: float32 [512, 256, 256], P('sub', 'shot')
The draws below stay inside these ranges and needn't reach their ends.
Inputs may be any that keep to these rules, and one draw needn't show every extreme that they name: `receiver_sub`: among the 1024 receivers of one device's aligned block of a shot, at most 64 lie in one slab, and exactly 64 in some slab.
All inputs are finite; a program needn't handle non-finite values.
Results may differ from the reference program's by a relative error of at most 0.0003.
Values sent between devices are 32-bit elements; how exact they have to be, the bound alone decides.
No kernel may reach another device: no remote copies, remote signals or barrier semaphores. Data moves between devices by JAX's collectives and lax.ppermute only.
A program may use at most 128 MiB of HBM per device.

```python
import math
import jax
import jax.numpy as jnp
import numpy as np

NY = 256
NZ = 256
PML = 16
STEPS = 4
REC_DEV = 1024
CAP = 64
SHOTS = 4
NX = 512
CELLS = 1048576
RECEIVERS = 32768
N_SUB = 32


def plant(drawn, own_key, least, top_value):
    spot = [jax.random.randint(jax.random.fold_in(own_key, axis), (), 0, length) for axis, length in enumerate(drawn.shape)]
    longest = drawn.shape.index(max(drawn.shape))
    next_to = spot[:longest] + [(spot[longest] + 1) % drawn.shape[longest]] + spot[longest + 1:]
    return drawn.at[tuple(spot)].set(least).at[tuple(next_to)].set(top_value)


def block_scale(stream_key, dims, shards, low, top_value):
    def one(position, blocks):
        heights = jax.random.uniform(jax.random.fold_in(jax.random.fold_in(stream_key, 6), position), (blocks,), jnp.float32, low / len(shards), top_value / len(shards))
        return jnp.repeat(jnp.exp(heights), dims[position] // blocks).reshape((-1,) + (1,) * (len(dims) - position - 1))

    loudness = one(*shards[0])
    for cut in shards[1:]:
        loudness = loudness * one(*cut)
    return loudness


def routed_block(stream_key, own, number, rows, number_of, top, limit, slope):
    order = jax.random.permutation(stream_key, number_of)
    heavy_load, usual = shares(number_of, rows * top, limit, slope, True), shares(number_of, rows * top, limit, slope, False)
    places = jnp.arange(number_of)

    def named(tallies, offset_by):
        used = int((tallies > 0).sum())
        fixed = max(1, used // 4)
        passed = fixed + (places - fixed + offset_by * (used - fixed)) % max(1, number_of - fixed)
        return jnp.zeros((number_of,), jnp.int32).at[order[jnp.where(places < fixed, places, passed)]].set(jnp.asarray(tallies, jnp.int32))

    tallies = jnp.where(number % 4 == 0, named(heavy_load, number // 4), named(usual, number - number // 4 - 1))
    mixed = jax.random.permutation(jax.random.fold_in(own, 3), number_of)
    giver, receiver = mixed[0:number_of // 2 * 2:2], mixed[1:number_of // 2 * 2:2]
    slack = jnp.minimum(tallies[giver] - 1, limit - tallies[receiver]) // 2
    slack = jnp.where((giver == order[0]) | (receiver == order[0]) | (tallies[receiver] == 0), 0, jnp.maximum(slack, 0))
    passed = jax.random.randint(jax.random.fold_in(own, 4), (number_of // 2,), 0, 1 << 20) % (slack + 1)
    tallies = tallies.at[giver].add(-passed).at[receiver].add(passed)
    members = jnp.searchsorted(jnp.cumsum(tallies), jnp.arange(rows * top), side="right").astype(jnp.int32)
    table = members.reshape(top, rows).T
    table = table[jax.random.permutation(jax.random.fold_in(own, 1), rows)]
    offset_by = jax.random.randint(jax.random.fold_in(own, 2), (rows, 1), 0, top)
    return jnp.take_along_axis(table, (jnp.arange(top)[None, :] + offset_by) % top, axis=1)


def shares(amount, total, most, skew, full):
    loads = [(1 << 20) // math.isqrt(standing ** skew) + 1 for standing in range(1, amount + 1)]
    largest = most if full else min(most, max(-(-total // amount), total * loads[0] // sum(loads)))
    least = 1 if total - largest >= amount - 1 else 0
    counts, rest = [largest] + [least] * (amount - 1), total - largest - least * (amount - 1)
    while rest > 0:
        free = [i for i in range(1, amount) if counts[i] < largest] or [i for i in range(1, amount) if counts[i] < most]
        mass, remaining = sum([loads[i] for i in free]), rest
        for i in free:
            addition = min(most - counts[i], max(1, remaining * loads[i] // mass), rest)
            counts[i] = counts[i] + addition
            rest = rest - addition
    return np.array(counts)


def scatter_about(rng, shape, scale, bound, shards=(), kind=jnp.bfloat16):
    factor_of = block_scale(rng, shape, shards, -0.22, 0.18) if shards else 1.0
    entries = jax.random.normal(rng, shape, jnp.float32) * scale * factor_of
    return jnp.minimum(jnp.maximum(entries, -bound), bound).astype(kind)


def setup_inputs(seed: int = 0) -> dict:
    keys = jax.random.split(jax.random.key(seed), 8)
    velocity = jnp.clip(jnp.exp(math.log(4.5) - 1.0986123 * jax.random.uniform(keys[0], (NX, NY, NZ), jnp.float32) ** block_scale(keys[0], (NX, NY, NZ), ((0, 32),), -0.2, 0.2)), 1.5, 4.5)
    adjoint_now = scatter_about(keys[1], (SHOTS, NX, NY, NZ), 0.25, 1.5, ((0, 4), (1, 32)), jnp.float32)
    adjoint_prev = scatter_about(keys[2], (SHOTS, NX, NY, NZ), 0.25, 1.5, ((0, 4), (1, 32)), jnp.float32)
    forward_accel = scatter_about(keys[3], (SHOTS, STEPS, NX, NY, NZ), 1.0, 6.0, ((0, 4), (2, 32)))
    traces = scatter_about(keys[4], (SHOTS, STEPS, RECEIVERS), 20.0, 120.0, ((0, 4), (2, 32)), jnp.float32)
    receiver_sub_keys = jax.random.split(jax.random.fold_in(keys[5], 1), SHOTS * RECEIVERS // REC_DEV)
    receiver_sub_turns = jax.random.permutation(jax.random.fold_in(keys[5], 3), SHOTS * RECEIVERS // REC_DEV)
    receiver_sub = jax.vmap(lambda own, number: routed_block(jax.random.fold_in(keys[5], 2), own, number, REC_DEV, N_SUB, 1, CAP, 2))(receiver_sub_keys, receiver_sub_turns).reshape((SHOTS, RECEIVERS, 1))
    receiver_cell = plant(jax.random.randint(keys[6], (SHOTS, RECEIVERS), 0, CELLS), jax.random.fold_in(keys[6], 1), 0, CELLS - 1).astype(jnp.int32)
    return {"velocity": velocity, "adjoint_now": adjoint_now, "adjoint_prev": adjoint_prev, "forward_accel": forward_accel, "traces": traces, "receiver_sub": receiver_sub, "receiver_cell": receiver_cell}


COEFFS = (-205.0 / 72.0, 8.0 / 5.0, -1.0 / 5.0, 8.0 / 315.0, -1.0 / 560.0)
COURANT = 0.09
DAMP_MAX = 0.3


def profile(index, count):
    depth = jnp.maximum(jnp.maximum(PML - index, index - (count - 1 - PML)), 0.0) / PML
    return depth * depth


def laplace(padded, field):
    size_x, size_y, size_z = field.shape
    total = 3.0 * COEFFS[0] * field
    for k in range(1, 5):
        total = total + COEFFS[k] * (
            padded[4 + k:4 + k + size_x, 4:4 + size_y, 4:4 + size_z]
            + padded[4 - k:4 - k + size_x, 4:4 + size_y, 4:4 + size_z]
            + padded[4:4 + size_x, 4 + k:4 + k + size_y, 4:4 + size_z]
            + padded[4:4 + size_x, 4 - k:4 - k + size_y, 4:4 + size_z]
            + padded[4:4 + size_x, 4:4 + size_y, 4 + k:4 + k + size_z]
            + padded[4:4 + size_x, 4:4 + size_y, 4 - k:4 - k + size_z])
    return total


def reference(velocity, adjoint_now, adjoint_prev, forward_accel, traces, receiver_sub, receiver_cell):
    coord_x = profile(jnp.arange(NX, dtype=jnp.float32), NX)
    coord_y = profile(jnp.arange(NY, dtype=jnp.float32), NY)
    coord_z = profile(jnp.arange(NZ, dtype=jnp.float32), NZ)
    damp = DAMP_MAX * (coord_x[:, None, None] + coord_y[None, :, None] + coord_z[None, None, :])
    speed_sq = (COURANT * velocity) ** 2
    weight = 2.0 / (velocity * velocity * velocity)
    gradient = jnp.zeros((NX, NY, NZ), jnp.float32)
    finals = []
    for shot_index in range(SHOTS):
        current = adjoint_now[shot_index]
        previous = adjoint_prev[shot_index]
        places = (receiver_sub[shot_index, :, 0] * CELLS + receiver_cell[shot_index]).astype(jnp.int32)
        for step in range(STEPS):
            source = jnp.zeros((NX * NY * NZ,), jnp.float32).at[places].add(traces[shot_index, step]).reshape(NX, NY, NZ)
            padded = jnp.pad(current, 4)
            after = (2.0 * current - (1.0 - damp) * previous + speed_sq * (laplace(padded, current) + source)) / (1.0 + damp)
            gradient = gradient + weight * after * forward_accel[shot_index, step].astype(jnp.float32)
            previous = current
            current = after
        finals.append(current)
    return jnp.stack(finals), gradient
```

```python
import functools

import jax
import jax.numpy as jnp
import ml_dtypes
import numpy as np
from jax import lax
from jax.experimental import pallas as pl
from jax.experimental.pallas import tpu as pltpu
from jax.sharding import PartitionSpec as P

PML = 16
STEPS = 4
COEFFS = (-205.0 / 72.0, 8.0 / 5.0, -1.0 / 5.0, 8.0 / 315.0, -1.0 / 560.0)
COURANT = 0.09
DAMP_MAX = 0.3
RATIO = tuple(c / COEFFS[1] for c in COEFFS)
SLAB = 16
SIZE = 256
HALF = 128
CAP = 64
MIB = 1 << 20

bf16 = jnp.bfloat16
f32 = jnp.float32


def params(mib, dims=1):
    return pltpu.CompilerParams(
        vmem_limit_bytes=mib * MIB, dimension_semantics=("arbitrary",) * dims if dims else None
    )


def cost(flops, mib):
    return pl.CostEstimate(flops=int(flops), bytes_accessed=int(mib * MIB), transcendentals=0)


def profile(index, count):
    depth = jnp.maximum(jnp.maximum(PML - index, index - (count - 1 - PML)), 0.0) / PML
    return depth * depth


def band():
    m = np.zeros((SIZE, SIZE), np.float32)
    for k in range(1, 5):
        m += RATIO[k] * (np.eye(SIZE, k=k, dtype=np.float32) + np.eye(SIZE, k=-k, dtype=np.float32))
    return m.astype(ml_dtypes.bfloat16)


def route_body(slabs, target_ref, cell_ref, trace_ref, out_ref, pick):
    listed = target_ref.shape[1]
    slots = slabs * CAP
    target = target_ref[...]
    hot = (lax.broadcasted_iota(jnp.int32, (slabs, listed), 0) == target).astype(bf16)
    earlier = (
        lax.broadcasted_iota(jnp.int32, (listed, listed), 0)
        < lax.broadcasted_iota(jnp.int32, (listed, listed), 1)
    ).astype(bf16)
    before = jnp.dot(hot, earlier, preferred_element_type=f32)
    rank = jnp.sum(before * hot.astype(f32), axis=0, keepdims=True)
    place = target * CAP + rank.astype(jnp.int32)
    value = trace_ref[...]
    top = value.astype(bf16)
    rest = value - top.astype(f32)
    middle = rest.astype(bf16)
    last = (rest - middle.astype(f32)).astype(bf16)
    cell = cell_ref[...]
    pieces = jnp.concatenate(
        [(cell >> 12).astype(f32), ((cell >> 4) & 255).astype(f32), (cell & 15).astype(f32), jnp.zeros((1, listed), f32)],
        axis=0,
    ).astype(bf16)
    table = jnp.concatenate([top, middle, last, pieces], axis=0)
    chunk = pick.shape[0]
    for start in range(0, slots, chunk):
        pick[...] = (
            lax.broadcasted_iota(jnp.int32, (chunk, listed), 0) + start == place
        ).astype(f32).astype(bf16)
        got = lax.dot_general(
            table, pick[...], (((1,), (1,)), ((), ())), preferred_element_type=f32
        )
        values = got[0:4] + got[4:8] + got[8:12]
        cells = got[12:13] * 4096.0 + got[13:14] * 16.0 + got[14:15]
        block = jnp.concatenate([values, jnp.broadcast_to(cells, (4, chunk))], axis=0)
        for j in range(chunk // CAP):
            out_ref[start // CAP + j] = block[:, j * CAP : (j + 1) * CAP]


def route(target, cell, trace, slabs):
    return pl.pallas_call(
        functools.partial(route_body, slabs),
        out_shape=jax.ShapeDtypeStruct((slabs, 8, CAP), f32),
        scratch_shapes=[pltpu.VMEM((256, target.shape[1]), bf16)],
        compiler_params=params(32, 0),
        cost_estimate=cost(2e8, 4),
        name="route",
    )(target, cell, trace)


def inject_body(cell_ref, value_ref, out_ref, dense):
    plane = pl.program_id(0)

    @pl.when(plane == 0)
    def _():
        zero = jnp.zeros((256, 128), f32)

        @pl.loop(0, dense.shape[0] // 256)
        def _(i):
            dense[pl.ds(pl.multiple_of(i * 256, 256), 256), :] = zero

        position = lax.broadcasted_iota(jnp.int32, (8, 128), 1) + 128 * (
            lax.broadcasted_iota(jnp.int32, (8, 128), 0) >> 2
        )
        batch = 4

        @pl.loop(0, value_ref.shape[0])
        def _(source):
            tile = value_ref[source]
            eight = jnp.concatenate([tile[0:4], tile[0:4]], axis=0)
            for first in range(0, CAP, batch):
                cells = [cell_ref[source * CAP + first + j] for j in range(batch)]
                rows = [c >> 8 for c in cells]
                add = [
                    jnp.where(position == (cells[j] & 255), eight[:, first + j : first + j + 1], 0.0)
                    for j in range(batch)
                ]
                at = [pl.ds(pl.multiple_of(r * 8, 8), 8) for r in rows]
                total = [dense[a, :] + u for a, u in zip(at, add)]
                for j in range(batch):
                    for i in range(j):
                        same = (rows[i] == rows[j]).astype(f32)
                        total[j] = total[j] + same * add[i]
                for j in range(batch):
                    dense[at[j], :] = total[j]

    @pl.loop(0, SIZE // 8)
    def _(group):
        base = (plane * SIZE + group * 8) * 8
        row = pl.ds(pl.multiple_of(group * 8, 8), 8)
        for step in range(STEPS):
            for half in range(2):
                out_ref[step, 0, row, half * HALF : (half + 1) * HALF] = dense[
                    pl.ds(base + half * 4 + step, 8, stride=8), :
                ]


def inject(cells, values):
    return pl.pallas_call(
        inject_body,
        out_shape=jax.ShapeDtypeStruct((STEPS, SLAB, SIZE, SIZE), f32),
        grid=(SLAB,),
        in_specs=[
            pl.BlockSpec(memory_space=pltpu.SMEM),
            pl.BlockSpec(values.shape, lambda i: (0, 0, 0)),
        ],
        out_specs=pl.BlockSpec((STEPS, 1, SIZE, SIZE), lambda i: (0, i, 0, 0)),
        scratch_shapes=[pltpu.VMEM((SLAB * SIZE * 8, 128), f32)],
        compiler_params=params(30),
        cost_estimate=cost(1e7, 32),
        name="inject",
    )(cells, values)


def side_of(group, parity):
    return (group + parity + 1) % 2


def first_edges_body(scalar_ref, *refs):
    for source, target in zip(refs[:4], refs[4:]):
        target[...] = source[...]


def first_edges(current, scalars):
    def source(group, half):
        return pl.BlockSpec((1, SIZE, HALF), lambda i, s: (side_of(group, s[0]) * 12 + i, 0, half))

    out = pl.BlockSpec((1, SIZE, HALF), lambda i, s: (i, 0, 0))
    order = [(group, half) for half in range(2) for group in range(2)]
    return pl.pallas_call(
        first_edges_body,
        out_shape=[jax.ShapeDtypeStruct((4, SIZE, HALF), f32)] * 4,
        grid_spec=pltpu.PrefetchScalarGridSpec(
            num_scalar_prefetch=1,
            grid=(4,),
            in_specs=[source(g, h) for g, h in order],
            out_specs=[out] * 4,
        ),
        compiler_params=params(8),
        cost_estimate=cost(1e5, 4),
        name="first_edges",
    )(scalars, current, current, current, current)


def factor(speed, damp):
    inverse = 1.0 / (1.0 + damp)
    return inverse, (COURANT * COURANT) * (speed * speed) * inverse


def local_body(step, scalar_ref, damp_x_ref, q_ref, p_ref, v_ref, s_ref, damp_ref, band_ref, *rest):
    if step < 2:
        n_ref, high, low, mixed = rest
    elif step == 2:
        a0_ref, a1_ref, n_ref, g_ref, high, low, mixed = rest
    else:
        a0_ref, a1_ref, part_ref, n_ref, loc_ref, send_ref, keep_ref, high, low, mixed, grad = rest
    plane = pl.program_id(0)
    here = q_ref[plane]
    top = here.astype(bf16)
    high[...] = top
    low[...] = (here - top.astype(f32)).astype(bf16)
    matrix = band_ref[...]
    mixed[...] = (
        jnp.dot(matrix, high[...], preferred_element_type=f32)
        + jnp.dot(matrix, low[...], preferred_element_type=f32)
        + jnp.dot(high[...], matrix, preferred_element_type=f32)
        + jnp.dot(low[...], matrix, preferred_element_type=f32)
    )
    damp_x = damp_x_ref[plane]
    rows = 16

    def update(row, across):
        now = q_ref[plane, row, :]
        before = p_ref[0, row, :]
        speed = v_ref[0, row, :]
        inverse, gain = factor(speed, damp_ref[row, :] + damp_x)
        around = mixed[row, :] + across(row)
        laplace = (3.0 * COEFFS[0]) * now + COEFFS[1] * around
        after = before + (2.0 * inverse) * (now - before) + gain * (laplace + s_ref[0, 0, row, :])
        n_ref[0, row, :] = after
        if step == 2:
            g_ref[0, row, :] = before * a0_ref[0, 0, 0, row, :].astype(f32) + now * a1_ref[0, 0, 0, row, :].astype(f32)
        if step == 3:
            total = (
                part_ref[0, row, :]
                + now * a0_ref[0, 0, 0, row, :].astype(f32)
                + after * a1_ref[0, 0, 0, row, :].astype(f32)
            )
            grad[row, :] = total * (2.0 / (speed * speed * speed))

    inside = jnp.logical_and(plane >= 4, plane < SLAB - 4)

    @pl.when(inside)
    def _():
        def across(row):
            total = q_ref[plane - 1, row, :] + q_ref[plane + 1, row, :]
            for k in range(2, 5):
                total = total + RATIO[k] * (q_ref[plane - k, row, :] + q_ref[plane + k, row, :])
            return total

        @pl.loop(0, SIZE // rows)
        def _(i):
            update(pl.ds(pl.multiple_of(i * rows, rows), rows), across)

    @pl.when(jnp.logical_not(inside))
    def _():
        terms = []
        for k in range(1, 5):
            for offset in (-k, k):
                at = plane + offset
                fits = jnp.logical_and(at >= 0, at < SLAB)
                terms.append((jnp.clip(at, 0, SLAB - 1), jnp.where(fits, RATIO[k], 0.0).astype(f32)))

        def across(row):
            total = terms[0][1] * q_ref[terms[0][0], row, :]
            for at, weight in terms[1:]:
                total = total + weight * q_ref[at, row, :]
            return total

        @pl.loop(0, SIZE // rows)
        def _(i):
            update(pl.ds(pl.multiple_of(i * rows, rows), rows), across)

    if step == 3:
        core = scalar_ref[1]

        @pl.when(inside)
        def _():
            for y in range(2):
                send_ref[0, y] = grad[pl.ds(pl.multiple_of(y * 128 + 64 * (1 - core), 64), 64), :]
                keep_ref[0, y] = grad[pl.ds(pl.multiple_of(y * 128 + 64 * core, 64), 64), :]

        @pl.when(jnp.logical_not(inside))
        def _():
            loc_ref[0] = grad[...]


def local_step(step, scalars, damp_x, q, p, v, s, damp, accel, part):
    plane = (1, SIZE, SIZE)
    plane_spec = pl.BlockSpec(plane, lambda i, *_: (i, 0, 0))
    whole_spec = pl.BlockSpec((SLAB, SIZE, SIZE), lambda i, *_: (0, 0, 0), pipeline_mode=pl.Buffered(1))
    flat_spec = pl.BlockSpec((SIZE, SIZE), lambda i, *_: (0, 0))
    in_specs = [
        whole_spec,
        plane_spec,
        plane_spec,
        pl.BlockSpec((1,) + plane, lambda i, *_: (step, i, 0, 0)),
        flat_spec,
        flat_spec,
    ]
    operands = [q, p, v, s, damp, jnp.asarray(band())]
    out_specs = [plane_spec]
    out_shape = [jax.ShapeDtypeStruct((SLAB, SIZE, SIZE), f32)]
    scratch = [
        pltpu.VMEM((SIZE, SIZE), bf16),
        pltpu.VMEM((SIZE, SIZE), bf16),
        pltpu.VMEM((SIZE, SIZE), f32),
    ]
    mib = 20

    def accel_spec(t):
        return pl.BlockSpec((1, 1) + plane, lambda i, *_: (0, t, i, 0, 0))

    if step == 2:
        in_specs += [accel_spec(0), accel_spec(1)]
        operands += [accel, accel]
        out_specs.append(plane_spec)
        out_shape.append(jax.ShapeDtypeStruct((SLAB, SIZE, SIZE), f32))
        mib = 28
    if step == 3:
        in_specs += [accel_spec(2), accel_spec(3), plane_spec]
        operands += [accel, accel, part]
        out_specs.append(
            pl.BlockSpec(plane, lambda i, *_: (jnp.where(i < 4, i, jnp.where(i < 12, 3, i - 8)), 0, 0))
        )
        out_shape.append(jax.ShapeDtypeStruct((8, SIZE, SIZE), f32))
        quarter = pl.BlockSpec((1, 2, 64, SIZE), lambda i, *_: (jnp.clip(i - 4, 0, 7), 0, 0, 0))
        out_specs += [quarter, quarter]
        out_shape += [jax.ShapeDtypeStruct((8, 2, 64, SIZE), f32)] * 2
        scratch.append(pltpu.VMEM((SIZE, SIZE), f32))
        mib = 33
    return pl.pallas_call(
        functools.partial(local_body, step),
        out_shape=out_shape,
        grid_spec=pltpu.PrefetchScalarGridSpec(
            num_scalar_prefetch=2,
            grid=(SLAB,),
            in_specs=in_specs,
            out_specs=out_specs,
            scratch_shapes=scratch,
        ),
        compiler_params=params(30),
        cost_estimate=cost(4e9, mib),
        name=f"local_step{step}",
    )(scalars, damp_x, *operands)


def edge_body(last, scalar_ref, damp_x_ref, even_ref, odd_ref, n_in, v_ref, damp_ref, *rest):
    if last:
        a_ref, loc_ref, n_ref, send_ref, keep_ref, grad = rest
    else:
        n_ref, e_ref, o_ref = rest
    group = pl.program_id(0)
    upper = side_of(group, scalar_ref[0])
    core = scalar_ref[1]
    rows = 16
    weights = [
        [
            jnp.where(
                upper == 1,
                COEFFS[4 + m - j] if m <= j else 0.0,
                COEFFS[4 + j - m] if m >= j else 0.0,
            ).astype(f32)
            for m in range(4)
        ]
        for j in range(4)
    ]

    def run(halo_ref, edge_ref):
        @pl.loop(0, HALF // rows)
        def _(i):
            row = pl.ds(pl.multiple_of(i * rows, rows), rows)
            halo = [halo_ref[m, row, :] for m in range(4)]
            damp = damp_ref[row, :]
            for j in range(4):
                speed = v_ref[j, row, :]
                _, gain = factor(speed, damp + damp_x_ref[upper * 12 + j])
                across = weights[j][0] * halo[0]
                for m in range(1, 4):
                    across = across + weights[j][m] * halo[m]
                extra = gain * across
                after = n_in[j, row, :] + extra
                n_ref[j, row, :] = after
                if last:
                    grad[j, row, :] = loc_ref[j, row, :] + extra * a_ref[0, 0, j, row, :].astype(f32) * (
                        2.0 / (speed * speed * speed)
                    )
                else:
                    edge_ref[j, row, :] = after

    @pl.when(group == 0)
    def _():
        run(even_ref, None if last else e_ref)

    @pl.when(group == 1)
    def _():
        run(odd_ref, None if last else o_ref)

    if last:
        send_ref[0, :, 0] = grad[:, pl.ds(pl.multiple_of(64 * (1 - core), 64), 64), :]
        keep_ref[0, :, 0] = grad[:, pl.ds(pl.multiple_of(64 * core, 64), 64), :]


def edge_step(last, half, scalars, damp_x, even, odd, n, v, damp, accel, loc):
    block = (4, HALF, HALF)

    def edge_block(g, y, s, _):
        return (3 * side_of(g, s[0]), y, half)

    edge_spec = pl.BlockSpec(block, edge_block)
    even_spec = pl.BlockSpec(block, lambda g, y, *_: (0, jnp.where(g == 0, y, 1), 0))
    odd_spec = pl.BlockSpec(block, lambda g, y, *_: (0, jnp.where(g == 0, 0, y), 0))
    in_specs = [
        even_spec,
        odd_spec,
        edge_spec,
        edge_spec,
        pl.BlockSpec((HALF, HALF), lambda g, y, *_: (y, half)),
    ]
    operands = [even, odd, n, v, damp]
    out_specs = [edge_spec]
    out_shape = [jax.ShapeDtypeStruct((SLAB, SIZE, SIZE), f32)]
    scratch = []
    if last:
        in_specs += [
            pl.BlockSpec((1, 1) + block, lambda g, y, s, _: (0, 3, 3 * side_of(g, s[0]), y, half)),
            pl.BlockSpec(block, lambda g, y, s, _: (side_of(g, s[0]), y, half)),
        ]
        operands += [accel, loc]
        quarter = pl.BlockSpec((1, 4, 1, 64, HALF), lambda g, y, *_: (g, 0, y, 0, 0))
        out_specs += [quarter, quarter]
        out_shape += [jax.ShapeDtypeStruct((2, 4, 2, 64, HALF), f32)] * 2
        scratch = [pltpu.VMEM(block, f32)]
    else:
        out_specs += [even_spec, odd_spec]
        out_shape += [jax.ShapeDtypeStruct((4, SIZE, HALF), f32)] * 2
    return pl.pallas_call(
        functools.partial(edge_body, last),
        out_shape=out_shape,
        grid_spec=pltpu.PrefetchScalarGridSpec(
            num_scalar_prefetch=2,
            grid=(2, 2),
            in_specs=in_specs,
            out_specs=out_specs,
            scratch_shapes=scratch,
        ),
        input_output_aliases={4: 0},
        compiler_params=params(16, 2),
        cost_estimate=cost(1e7, 7),
        name=f"edge_step{half}",
    )(scalars, damp_x, *operands)


def split_body(scalar_ref, got_ref, own_ref, send_ref, keep_ref):
    y = scalar_ref[2]
    send_ref[0] = got_ref[0, 1 - y] + own_ref[0, 1 - y]
    keep_ref[0] = got_ref[0, y] + own_ref[0, y]


def split_sum(scalars, got, own):
    layers, _, rows, width = got.shape
    step = pl.BlockSpec((1, 2, rows, width), lambda i, s: (i, 0, 0, 0))
    out = pl.BlockSpec((1, rows, width), lambda i, s: (i, 0, 0))
    return pl.pallas_call(
        split_body,
        out_shape=[jax.ShapeDtypeStruct((layers, rows, width), f32)] * 2,
        grid_spec=pltpu.PrefetchScalarGridSpec(
            num_scalar_prefetch=1, grid=(layers,), in_specs=[step, step], out_specs=[out, out]
        ),
        compiler_params=params(8),
        cost_estimate=cost(1e5, 3),
        name="split_sum",
    )(scalars, got, own)


def gather_body(scalar_ref, *refs):
    inner_a, inner_b, first_a, first_b, second_a, second_b, out_ref = refs
    block = pl.program_id(0)
    inside = jnp.logical_or(block == 1, block == 2)

    @pl.when(inside)
    def _():
        out_ref[...] = inner_a[...] + inner_b[...]

    @pl.when(jnp.logical_not(inside))
    def _():
        out_ref[:, :, 0:HALF] = first_a[...] + first_b[...]
        out_ref[:, :, HALF:SIZE] = second_a[...] + second_b[...]


def gather_sum(scalars, inner, first, second):
    inner_spec = pl.BlockSpec((4, 64, SIZE), lambda i, s: (jnp.clip(i - 1, 0, 1), 0, 0))

    def group(i, s):
        upper = (i == 3).astype(jnp.int32)
        return (upper + s[0] + 1) % 2, 0, 0

    edge_spec = pl.BlockSpec((4, 64, HALF), group)
    return pl.pallas_call(
        gather_body,
        out_shape=jax.ShapeDtypeStruct((SLAB, 64, SIZE), f32),
        grid_spec=pltpu.PrefetchScalarGridSpec(
            num_scalar_prefetch=1,
            grid=(4,),
            in_specs=[inner_spec, inner_spec] + [edge_spec] * 4,
            out_specs=pl.BlockSpec((4, 64, SIZE), lambda i, s: (i, 0, 0)),
        ),
        compiler_params=params(8),
        cost_estimate=cost(1e5, 3),
        name="gather_sum",
    )(scalars, *inner, *first, *second)


def shards(velocity, adjoint_now, adjoint_prev, forward_accel, traces, receiver_sub, receiver_cell):
    slabs = lax.axis_size("sub")
    slab = lax.axis_index("sub")
    shot = lax.axis_index("shot")
    pairs_even = [(i, i ^ 1) for i in range(slabs)]
    pairs_odd = [pair for a in range(1, slabs - 1, 2) for pair in ((a, a + 1), (a + 1, a))]
    shots = lax.axis_size("shot")
    swap_core = [(i, i ^ 1) for i in range(shots)]
    swap_row = [(i, i ^ 2) for i in range(shots)]
    scalars = jnp.stack([slab % 2, shot % 2, shot // 2]).astype(jnp.int32)
    start_x = (slab * SLAB).astype(f32)
    damp_x = DAMP_MAX * profile(start_x + jnp.arange(SLAB, dtype=f32), SLAB * slabs)
    line = profile(jnp.arange(SIZE, dtype=f32), SIZE)
    damp = DAMP_MAX * (line[:, None] + line[None, :])

    def exchange(even, odd):
        return lax.ppermute(even, "sub", pairs_even), lax.ppermute(odd, "sub", pairs_odd)

    current = adjoint_now[0]
    previous = adjoint_prev[0]
    even_a, odd_a, even_b, odd_b = first_edges(current, scalars)
    arrived_a = exchange(even_a, odd_a)
    arrived_b = exchange(even_b, odd_b)

    listed = receiver_sub.shape[1]
    sent = route(
        receiver_sub.reshape(1, listed), receiver_cell.reshape(1, listed), traces[0], slabs
    )
    got = lax.all_to_all(sent, "sub", split_axis=0, concat_axis=0, tiled=True)
    cells = got[:, 4, :].reshape(slabs * CAP).astype(jnp.int32)
    source = inject(cells, got)

    part = None
    for step in range(STEPS):
        out = local_step(
            step, scalars, damp_x, current, previous, velocity, source, damp, forward_accel, part
        )
        after = out[0]
        last = step == STEPS - 1
        loc = None
        if step == 2:
            part = out[1]
        if last:
            loc, send, keep = out[1:]
            send, inner_keep = split_sum(scalars, lax.ppermute(send, "shot", swap_core), keep)
            inner = (lax.ppermute(send, "shot", swap_row), inner_keep)
        outs = []
        for half, arrived in enumerate((arrived_a, arrived_b)):
            after, x, y = edge_step(
                last, half, scalars, damp_x, *arrived, after, velocity, damp, forward_accel, loc
            )
            if last:
                x = x.reshape(8, 2, 64, HALF)
                y = y.reshape(8, 2, 64, HALF)
                send, edge_keep = split_sum(scalars, lax.ppermute(x, "shot", swap_core), y)
                outs.append((lax.ppermute(send, "shot", swap_row), edge_keep))
            else:
                outs.append(exchange(x, y))
        previous = current
        current = after
        if not last:
            arrived_a, arrived_b = outs
    share = gather_sum(scalars, inner, *outs)
    return current[None], share


def solution(mesh):
    in_specs = (
        P("sub", None, None),
        P("shot", "sub", None, None),
        P("shot", "sub", None, None),
        P("shot", None, "sub", None, None),
        P("shot", None, "sub"),
        P("shot", "sub", None),
        P("shot", "sub"),
    )
    out_specs = (P("shot", "sub", None, None), P("sub", "shot", None))
    return jax.shard_map(shards, mesh=mesh, in_specs=in_specs, out_specs=out_specs, check_vma=False)
```

```python
import functools

import jax
import jax.numpy as jnp
import ml_dtypes
import numpy as np
from jax import lax
from jax.experimental import pallas as pl
from jax.experimental.pallas import tpu as pltpu
from jax.sharding import PartitionSpec as P

PML = 16
STEPS = 4
COEFFS = (-205.0 / 72.0, 8.0 / 5.0, -1.0 / 5.0, 8.0 / 315.0, -1.0 / 560.0)
COURANT = 0.09
DAMP_MAX = 0.3
RATIO = tuple(c / COEFFS[1] for c in COEFFS)
SLAB = 16
SIZE = 256
HALF = 128
CAP = 64
MIB = 1 << 20

bf16 = jnp.bfloat16
f32 = jnp.float32
VMEM = pl.BlockSpec(memory_space=pltpu.VMEM)
SMEM = pl.BlockSpec(memory_space=pltpu.SMEM)
ANY = pl.BlockSpec(memory_space=pl.ANY)


def params(mib, dims=1):
    return pltpu.CompilerParams(
        vmem_limit_bytes=mib * MIB, dimension_semantics=("arbitrary",) * dims if dims else None
    )


def pinned(x):
    return pltpu.with_memory_space_constraint(x, pltpu.VMEM)


def in_hbm(x):
    return pltpu.with_memory_space_constraint(x, pltpu.HBM)


def cost(flops, mib):
    return pl.CostEstimate(flops=int(flops), bytes_accessed=int(mib * MIB), transcendentals=0)


def profile(index, count):
    depth = jnp.maximum(jnp.maximum(PML - index, index - (count - 1 - PML)), 0.0) / PML
    return depth * depth


def band():
    m = np.zeros((SIZE, SIZE), np.float32)
    for k in range(1, 5):
        m += RATIO[k] * (np.eye(SIZE, k=k, dtype=np.float32) + np.eye(SIZE, k=-k, dtype=np.float32))
    return m.astype(ml_dtypes.bfloat16)


def route_body(slabs, target_ref, cell_ref, trace_ref, out_ref, pick):
    listed = target_ref.shape[1]
    slots = slabs * CAP
    target = target_ref[...]
    hot = (lax.broadcasted_iota(jnp.int32, (slabs, listed), 0) == target).astype(bf16)
    earlier = (
        lax.broadcasted_iota(jnp.int32, (listed, listed), 0)
        < lax.broadcasted_iota(jnp.int32, (listed, listed), 1)
    ).astype(bf16)
    before = jnp.dot(hot, earlier, preferred_element_type=f32)
    rank = jnp.sum(before * hot.astype(f32), axis=0, keepdims=True)
    place = target * CAP + rank.astype(jnp.int32)
    value = trace_ref[...]
    top = value.astype(bf16)
    rest = value - top.astype(f32)
    middle = rest.astype(bf16)
    last = (rest - middle.astype(f32)).astype(bf16)
    cell = cell_ref[...]
    pieces = jnp.concatenate(
        [(cell >> 12).astype(f32), ((cell >> 4) & 255).astype(f32), (cell & 15).astype(f32), jnp.zeros((1, listed), f32)],
        axis=0,
    ).astype(bf16)
    table = jnp.concatenate([top, middle, last, pieces], axis=0)
    out_ref[...] = jnp.zeros_like(out_ref)
    chunk = pick.shape[0]
    for start in range(0, slots, chunk):
        pick[...] = (
            lax.broadcasted_iota(jnp.int32, (chunk, listed), 0) + start == place
        ).astype(f32).astype(bf16)
        got = lax.dot_general(
            table, pick[...], (((1,), (1,)), ((), ())), preferred_element_type=f32
        )
        values = got[0:4] + got[4:8] + got[8:12]
        cells = got[12:13] * 4096.0 + got[13:14] * 16.0 + got[14:15]
        block = jnp.concatenate([values, jnp.broadcast_to(cells, (4, chunk))], axis=0)
        for j in range(chunk // CAP):
            out_ref[start // CAP + j, :, 0:CAP] = block[:, j * CAP : (j + 1) * CAP]


def route(target, cell, trace, slabs):
    return pl.pallas_call(
        functools.partial(route_body, slabs),
        out_shape=jax.ShapeDtypeStruct((slabs, 8, 128), f32),
        scratch_shapes=[pltpu.VMEM((256, target.shape[1]), bf16)],
        compiler_params=params(10, 0),
        cost_estimate=cost(1, 0),
        name="route",
    )(target, cell, trace)


def inject_body(value_ref, dense, cells_vmem, cell_ref, sem):
    cells_vmem[...] = value_ref[:, 4, :].astype(jnp.int32)
    copy = pltpu.make_async_copy(cells_vmem, cell_ref, sem)
    copy.start()
    zero = jnp.zeros((256, 128), f32)

    @pl.loop(0, dense.shape[0] // 256)
    def _(i):
        dense[pl.ds(pl.multiple_of(i * 256, 256), 256), :] = zero

    copy.wait()
    position = lax.broadcasted_iota(jnp.int32, (8, 128), 1) + 128 * (
        lax.broadcasted_iota(jnp.int32, (8, 128), 0) >> 2
    )
    batch = 4

    @pl.loop(0, value_ref.shape[0])
    def _(source):
        tile = value_ref[source]
        eight = jnp.concatenate([tile[0:4], tile[0:4]], axis=0)

        def some(first):
            cells = [cell_ref[source, first + j] for j in range(batch)]
            rows = [c >> 8 for c in cells]
            add = [
                jnp.where(position == (c & 255), eight[:, first + j : first + j + 1], 0.0)
                for j, c in enumerate(cells)
            ]
            at = [pl.ds(pl.multiple_of(r * 8, 8), 8) for r in rows]
            total = [dense[a, :] + u for a, u in zip(at, add)]
            for j in range(batch):
                for i in range(j):
                    same = (rows[i] == rows[j]).astype(f32)
                    total[j] = total[j] + same * add[i]
            for j in range(batch):
                dense[at[j], :] = total[j]

        for first in range(0, CAP, batch):
            some(first)


def source_of(dense, plane, start, step):
    base = (plane * SIZE + start) * 8 + step
    return jnp.concatenate([dense[pl.ds(base + half * 4, 8, stride=8), :] for half in range(2)], axis=1)


def inject(values):
    return pl.pallas_call(
        inject_body,
        out_shape=pltpu.VMEM((SLAB * SIZE * 8, 128), f32),
        in_specs=[VMEM],
        out_specs=VMEM,
        scratch_shapes=[
            pltpu.VMEM((values.shape[0], 128), jnp.int32),
            pltpu.SMEM((values.shape[0], 128), jnp.int32),
            pltpu.SemaphoreType.DMA,
        ],
        compiler_params=params(4, 0),
        cost_estimate=cost(1, 0),
        name="inject",
    )(values)


def side_of(group, parity):
    return (group + parity + 1) % 2


def first_edges_body(scalar_ref, source, *refs):
    sems = refs[4]
    copies = []
    for i in range(4):
        half, group = divmod(i, 2)
        start = 12 * side_of(group, scalar_ref[0])
        copies.append(
            pltpu.make_async_copy(
                source.at[pl.ds(start, 4), :, pl.ds(half * HALF, HALF)], refs[i], sems.at[i]
            )
        )
    for copy in copies:
        copy.start()
    for copy in copies:
        copy.wait()


def first_edges(current, scalars):
    return pl.pallas_call(
        first_edges_body,
        out_shape=[jax.ShapeDtypeStruct((4, SIZE, HALF), f32)] * 4,
        in_specs=[SMEM, ANY],
        out_specs=[VMEM] * 4,
        scratch_shapes=[pltpu.SemaphoreType.DMA((4,))],
        compiler_params=params(4, 0),
        cost_estimate=cost(1, 0),
        name="first_edges",
    )(scalars, in_hbm(current))


def factor(speed, damp):
    inverse = 1.0 / (1.0 + damp)
    return inverse, (COURANT * COURANT) * (speed * speed) * inverse


def local_body(step, scalar_ref, damp_x_ref, q_hbm, p_hbm, v_hbm, s_ref, damp_ref, band_ref, *rest):
    if step < 2:
        n_hbm, edge_ref, gain_ref, *scratch = rest
    elif step == 2:
        accel_hbm, n_hbm, edge_ref, gain_ref, part_hbm, *scratch = rest
    else:
        accel_hbm, part_hbm, n_hbm, loc_ref, *scratch = rest
        (send_ref, keep_ref), scratch = scratch[:2], scratch[2:]
    high, low, mixed0, mixed1, q_ref, n_ref, v_ref, load_sems, store_sems = scratch[:9]
    if step >= 2:
        accel, accel_sems, part, part_sems = scratch[9:13]
    if step == 3:
        shared = scratch[13]
    p_ref = n_ref
    mixed = (mixed0, mixed1)
    group_size = 4
    groups = SLAB // group_size
    span = SIZE // group_size
    rows = 8 if step < 2 else 16
    core = scalar_ref[1]
    first = 0 if step == 2 else 2

    def planes(group):
        return pl.ds(group_size * group, group_size)

    def load(i, group):
        source, target = ((q_hbm, q_ref), (v_hbm, v_ref), (p_hbm, p_ref))[i]
        return pltpu.make_async_copy(
            source.at[planes(group)], target.at[planes(group)], load_sems.at[i, group]
        )

    def fetch(group):
        return pltpu.make_async_copy(
            accel_hbm.at[0, pl.ds(first, 2), planes(group)], accel.at[group], accel_sems.at[group]
        )

    def load_part(group):
        return pltpu.make_async_copy(
            part_hbm.at[planes(group)], part.at[planes(group)], part_sems.at[group]
        )

    def stores(group):
        out = [pltpu.make_async_copy(n_ref.at[planes(group)], n_hbm.at[planes(group)], store_sems.at[group])]
        if step == 2:
            out.append(
                pltpu.make_async_copy(
                    part.at[planes(group)], part_hbm.at[planes(group)], part_sems.at[group]
                )
            )
        return out

    def others(group):
        out = [load(1, group), load(2, group)]
        if step >= 2:
            out.append(fetch(group))
        if step == 3:
            out.append(load_part(group))
        return out

    load(0, 0).start()
    for group in range(groups):
        if group + 1 < groups:
            load(0, group + 1).start()
        for copy in others(group):
            copy.start()
    load(0, 0).wait()

    def prepare(plane, into):
        here = q_ref[plane]
        top = here.astype(bf16)
        high[...] = top
        low[...] = (here - top.astype(f32)).astype(bf16)
        matrix = band_ref[...]
        into[...] = (
            jnp.dot(high[...], matrix, preferred_element_type=f32)
            + jnp.dot(low[...], matrix, preferred_element_type=f32)
            + jnp.dot(matrix, high[...], preferred_element_type=f32)
            + jnp.dot(matrix, low[...], preferred_element_type=f32)
        )

    def update(group, whole, offset):
        start = pl.multiple_of(whole + offset, rows)
        row = pl.ds(start, rows)
        lowest = group_size * group
        field = {x: q_ref[x, row, :] for x in range(max(0, lowest - 4), min(SLAB, lowest + group_size + 4))}
        damp = damp_ref[row, :]
        for plane in range(lowest, lowest + group_size):

            def rate(t):
                return accel[group, t, plane - lowest, row, :].astype(f32)

            around = mixed[group % 2][plane - lowest, row, :]
            for k in range(1, 5):
                both = [field[x] for x in (plane - k, plane + k) if 0 <= x < SLAB]
                term = both[0] if len(both) == 1 else both[0] + both[1]
                around = around + (term if k == 1 else RATIO[k] * term)
            now = field[plane]
            before = p_ref[plane, row, :]
            speed = v_ref[plane, row, :]
            inverse, gain = factor(speed, damp + damp_x_ref[plane])
            laplace = (3.0 * COEFFS[0]) * now + COEFFS[1] * around
            laplace = laplace + jnp.concatenate(
                [source_of(s_ref, plane, start + i * 8, step) for i in range(rows // 8)], axis=0
            )
            after = before + (2.0 * inverse) * (now - before) + gain * laplace
            n_ref[plane, row, :] = after
            if step == 2:
                part[plane, row, :] = before * rate(0) + now * rate(1)
            if step == 3:
                total = part[plane, row, :] + now * rate(0) + after * rate(1)
                grad = total * (2.0 / (speed * speed * speed))
                if plane < 4 or plane >= SLAB - 4:
                    loc_ref[plane if plane < 4 else plane - 8, row, :] = grad
                else:
                    shared[plane - lowest, pl.ds(start - whole, rows), :] = grad
            elif plane < 4 or plane >= SLAB - 4:
                edge_ref[plane if plane < 4 else plane - 8, row, :] = after
                gain_ref[plane if plane < 4 else plane - 8, row, :] = gain

    for plane in range(group_size):
        prepare(plane, mixed0.at[plane])
    for group in range(groups):
        if group + 1 < groups:
            load(0, group + 1).wait()
        for copy in others(group):
            copy.wait()

        @pl.loop(0, group_size)
        def _(j):
            if group + 1 < groups:
                prepare(group_size * (group + 1) + j, mixed[(group + 1) % 2].at[j])
            for i in range(span // rows):
                update(group, j * span, i * rows)
            if step == 3 and 0 < group < groups - 1:
                inner = pl.ds(group_size * (group - 1), group_size)

                @pl.when((j & 1) == core)
                def _():
                    keep_ref[inner, j >> 1] = shared[...]

                @pl.when((j & 1) != core)
                def _():
                    send_ref[inner, j >> 1] = shared[...]

        for copy in stores(group):
            copy.start()
    for group in range(groups):
        for copy in stores(group):
            copy.wait()


def local_step(step, scalars, damp_x, q, p, v, s, damp, accel, part=None):
    whole = (SLAB, SIZE, SIZE)
    in_specs = [SMEM, SMEM] + [ANY] * 3 + [VMEM] * 3
    operands = [scalars, damp_x, in_hbm(q), in_hbm(p), in_hbm(v), pinned(s), damp, jnp.asarray(band())]
    out_specs = [ANY]
    out_shape = [pltpu.HBM(whole, f32)]
    scratch = [
        pltpu.VMEM((SIZE, SIZE), bf16),
        pltpu.VMEM((SIZE, SIZE), bf16),
        pltpu.VMEM((4, SIZE, SIZE), f32),
        pltpu.VMEM((4, SIZE, SIZE), f32),
        pltpu.VMEM(whole, f32),
        pltpu.VMEM(whole, f32),
        pltpu.VMEM(whole, f32),
        pltpu.SemaphoreType.DMA((3, 4)),
        pltpu.SemaphoreType.DMA((4,)),
    ]
    if step >= 2:
        in_specs.append(ANY)
        operands.append(in_hbm(accel))
        scratch += [
            pltpu.VMEM((4, 2, 4, SIZE, SIZE), bf16),
            pltpu.SemaphoreType.DMA((4,)),
            pltpu.VMEM(whole, f32),
            pltpu.SemaphoreType.DMA((4,)),
        ]
    if step < 3:
        out_specs += [VMEM] * 2
        out_shape += [jax.ShapeDtypeStruct((8, SIZE, SIZE), f32)] * 2
    if step == 2:
        out_specs.append(ANY)
        out_shape.append(pltpu.HBM(whole, f32))
    if step == 3:
        in_specs.append(ANY)
        operands.append(in_hbm(part))
        out_specs += [VMEM] * 3
        out_shape.append(jax.ShapeDtypeStruct((8, SIZE, SIZE), f32))
        out_shape += [jax.ShapeDtypeStruct((8, 2, 64, SIZE), f32)] * 2
        scratch.append(pltpu.VMEM((4, 64, SIZE), f32))
    return pl.pallas_call(
        functools.partial(local_body, step),
        out_shape=out_shape,
        in_specs=in_specs,
        out_specs=out_specs,
        scratch_shapes=scratch,
        compiler_params=params(24, 0),
        cost_estimate=cost(4e9, 20),
        name=f"local_step{step}",
    )(*operands)


def halo_weights(upper):
    return [
        [
            jnp.where(
                upper == 1,
                COEFFS[4 + m - j] if m <= j else 0.0,
                COEFFS[4 + j - m] if m >= j else 0.0,
            ).astype(f32)
            for m in range(4)
        ]
        for j in range(4)
    ]


def edge_body(half, scalar_ref, even_ref, odd_ref, edge_ref, gain_ref, _, n_hbm, e_ref, o_ref, sems):
    rows = 16
    lanes = slice(half * HALF, (half + 1) * HALF)
    copies = []
    for group in range(2):
        upper = side_of(group, scalar_ref[0])
        halo_ref, out_ref = ((even_ref, e_ref), (odd_ref, o_ref))[group]
        weights = halo_weights(upper)

        @pl.loop(0, SIZE // rows)
        def _(i):
            row = pl.ds(pl.multiple_of(i * rows, rows), rows)
            halo = [halo_ref[m, row, :] for m in range(4)]
            for j in range(4):
                across = weights[j][0] * halo[0]
                for m in range(1, 4):
                    across = across + weights[j][m] * halo[m]
                layer = upper * 4 + j
                out_ref[j, row, :] = edge_ref[layer, row, lanes] + gain_ref[layer, row, lanes] * across

        copies.append(
            pltpu.make_async_copy(
                out_ref, n_hbm.at[pl.ds(12 * upper, 4), :, pl.ds(half * HALF, HALF)], sems.at[group]
            )
        )
        copies[-1].start()
    for copy in copies:
        copy.wait()


def edge_step(half, scalars, even, odd, edge, gain, n):
    return pl.pallas_call(
        functools.partial(edge_body, half),
        out_shape=[pltpu.HBM((SLAB, SIZE, SIZE), f32)] + [jax.ShapeDtypeStruct((4, SIZE, HALF), f32)] * 2,
        in_specs=[SMEM] + [VMEM] * 4 + [ANY],
        out_specs=[ANY, VMEM, VMEM],
        scratch_shapes=[pltpu.SemaphoreType.DMA((2,))],
        input_output_aliases={5: 0},
        compiler_params=params(12, 0),
        cost_estimate=cost(1, 0),
        name=f"edge_step{half}",
    )(scalars, even, odd, edge, gain, in_hbm(n))


def last_edge_body(
    scalar_ref, damp_x_ref, even_ref, odd_ref, n_in, v_ref, damp_ref, a_ref, loc_ref, n_ref, send_ref, keep_ref, grad
):
    group = pl.program_id(0)
    upper = side_of(group, scalar_ref[0])
    core = scalar_ref[1]
    rows = 16
    weights = halo_weights(upper)

    def run(halo_ref):
        @pl.loop(0, HALF // rows)
        def _(i):
            row = pl.ds(pl.multiple_of(i * rows, rows), rows)
            halo = [halo_ref[m, row, :] for m in range(4)]
            damp = damp_ref[row, :]
            for j in range(4):
                speed = v_ref[j, row, :]
                _, gain = factor(speed, damp + damp_x_ref[upper * 12 + j])
                across = weights[j][0] * halo[0]
                for m in range(1, 4):
                    across = across + weights[j][m] * halo[m]
                extra = gain * across
                after = n_in[j, row, :] + extra
                n_ref[j, row, :] = after
                grad[j, row, :] = loc_ref[j, row, :] + extra * a_ref[0, 0, j, row, :].astype(f32) * (
                    2.0 / (speed * speed * speed)
                )

    @pl.when(group == 0)
    def _():
        run(even_ref)

    @pl.when(group == 1)
    def _():
        run(odd_ref)

    send_ref[0, :, 0] = grad[:, pl.ds(pl.multiple_of(64 * (1 - core), 64), 64), :]
    keep_ref[0, :, 0] = grad[:, pl.ds(pl.multiple_of(64 * core, 64), 64), :]


def last_edge_step(half, scalars, damp_x, even, odd, n, v, damp, accel, loc):
    block = (4, HALF, HALF)

    def edge_block(g, y, s, _):
        return (3 * side_of(g, s[0]), y, half)

    edge_spec = pl.BlockSpec(block, edge_block)
    in_specs = [
        pl.BlockSpec(block, lambda g, y, *_: (0, jnp.where(g == 0, y, 1), 0)),
        pl.BlockSpec(block, lambda g, y, *_: (0, jnp.where(g == 0, 0, y), 0)),
        edge_spec,
        edge_spec,
        pl.BlockSpec((HALF, HALF), lambda g, y, *_: (y, half)),
        pl.BlockSpec((1, 1) + block, lambda g, y, s, _: (0, 3, 3 * side_of(g, s[0]), y, half)),
        pl.BlockSpec(block, lambda g, y, s, _: (side_of(g, s[0]), y, half)),
    ]
    quarter = pl.BlockSpec((1, 4, 1, 64, HALF), lambda g, y, *_: (g, 0, y, 0, 0))
    return pl.pallas_call(
        last_edge_body,
        out_shape=[jax.ShapeDtypeStruct((SLAB, SIZE, SIZE), f32)]
        + [jax.ShapeDtypeStruct((2, 4, 2, 64, HALF), f32)] * 2,
        grid_spec=pltpu.PrefetchScalarGridSpec(
            num_scalar_prefetch=2,
            grid=(2, 2),
            in_specs=in_specs,
            out_specs=[edge_spec, quarter, quarter],
            scratch_shapes=[pltpu.VMEM(block, f32)],
        ),
        input_output_aliases={4: 0},
        compiler_params=params(7, 2),
        cost_estimate=cost(1, 0),
        name=f"last_edge_step{half}",
    )(scalars, damp_x, even, odd, in_hbm(n), in_hbm(v), damp, in_hbm(accel), loc)


def split_body(scalar_ref, got_ref, own_ref, send_ref, keep_ref):
    y = scalar_ref[2]
    send_ref[0] = got_ref[0, 1 - y] + own_ref[0, 1 - y]
    keep_ref[0] = got_ref[0, y] + own_ref[0, y]


def split_sum(scalars, got, own):
    layers, _, rows, width = got.shape
    step = pl.BlockSpec((1, 2, rows, width), lambda i, s: (i, 0, 0, 0))
    out = pl.BlockSpec((1, rows, width), lambda i, s: (i, 0, 0))
    return pl.pallas_call(
        split_body,
        out_shape=[jax.ShapeDtypeStruct((layers, rows, width), f32)] * 2,
        grid_spec=pltpu.PrefetchScalarGridSpec(
            num_scalar_prefetch=1, grid=(layers,), in_specs=[step, step], out_specs=[out, out]
        ),
        compiler_params=params(4),
        cost_estimate=cost(1, 0),
        name="split_sum",
    )(scalars, got, own)


def gather_body(scalar_ref, *refs):
    inner_a, inner_b, first_a, first_b, second_a, second_b, out_ref = refs
    block = pl.program_id(0)
    inside = jnp.logical_or(block == 1, block == 2)

    @pl.when(inside)
    def _():
        out_ref[...] = inner_a[...] + inner_b[...]

    @pl.when(jnp.logical_not(inside))
    def _():
        out_ref[:, :, 0:HALF] = first_a[...] + first_b[...]
        out_ref[:, :, HALF:SIZE] = second_a[...] + second_b[...]


def gather_sum(scalars, inner, first, second):
    inner_spec = pl.BlockSpec((4, 64, SIZE), lambda i, s: (jnp.clip(i - 1, 0, 1), 0, 0))

    def group(i, s):
        upper = (i == 3).astype(jnp.int32)
        return (upper + s[0] + 1) % 2, 0, 0

    edge_spec = pl.BlockSpec((4, 64, HALF), group)
    return pl.pallas_call(
        gather_body,
        out_shape=jax.ShapeDtypeStruct((SLAB, 64, SIZE), f32),
        grid_spec=pltpu.PrefetchScalarGridSpec(
            num_scalar_prefetch=1,
            grid=(4,),
            in_specs=[inner_spec] * 2 + [edge_spec] * 4,
            out_specs=pl.BlockSpec((4, 64, SIZE), lambda i, s: (i, 0, 0)),
        ),
        compiler_params=params(4),
        cost_estimate=cost(1, 0),
        name="gather_sum",
    )(scalars, *inner, *first, *second)


def shards(velocity, adjoint_now, adjoint_prev, forward_accel, traces, receiver_sub, receiver_cell):
    slabs = lax.axis_size("sub")
    slab = lax.axis_index("sub")
    shot = lax.axis_index("shot")
    pairs_even = [(i, i ^ 1) for i in range(slabs)]
    pairs_odd = [pair for a in range(1, slabs - 1, 2) for pair in ((a, a + 1), (a + 1, a))]
    shots = lax.axis_size("shot")
    swap_core = [(i, i ^ 1) for i in range(shots)]
    swap_row = [(i, i ^ 2) for i in range(shots)]
    scalars = jnp.stack([slab % 2, shot % 2, shot // 2]).astype(jnp.int32)
    start_x = (slab * SLAB).astype(f32)
    damp_x = DAMP_MAX * profile(start_x + jnp.arange(SLAB, dtype=f32), SLAB * slabs)
    line = profile(jnp.arange(SIZE, dtype=f32), SIZE)
    damp = DAMP_MAX * (line[:, None] + line[None, :])

    def exchange(even, odd):
        return lax.ppermute(even, "sub", pairs_even), lax.ppermute(odd, "sub", pairs_odd)

    even_a, odd_a, even_b, odd_b = first_edges(adjoint_now[0], scalars)
    arrived_a = exchange(even_a, odd_a)
    arrived_b = exchange(even_b, odd_b)

    listed = receiver_sub.shape[1]
    sent = route(
        receiver_sub.reshape(1, listed), receiver_cell.reshape(1, listed), traces[0], slabs
    )
    got = lax.all_to_all(sent, "sub", split_axis=0, concat_axis=0, tiled=True)

    source = inject(got)

    current = adjoint_now[0]
    previous = adjoint_prev[0]
    part = []
    for step in range(STEPS):
        last = step == STEPS - 1
        after, *extra = local_step(
            step, scalars, damp_x, current, previous, velocity, source, damp, forward_accel, *part
        )
        outs = []
        if last:
            loc, inner_send, inner_keep = extra
            arrived_a, arrived_b = lax.optimization_barrier((arrived_a, arrived_b))
        else:
            edge, gain, *part = extra
        for half, arrived in enumerate((arrived_a, arrived_b)):
            if last:
                after, x, y = last_edge_step(
                    half, scalars, damp_x, *arrived, after, velocity, damp, forward_accel, loc
                )
                if half == 0:
                    inner_send, x = lax.optimization_barrier((inner_send, x))
                    send, inner_keep = split_sum(scalars, lax.ppermute(inner_send, "shot", swap_core), inner_keep)
                    send, after = lax.optimization_barrier((send, after))
                    inner = (lax.ppermute(send, "shot", swap_row), inner_keep)
                x = x.reshape(8, 2, 64, HALF)
                y = y.reshape(8, 2, 64, HALF)
                send, edge_keep = split_sum(scalars, lax.ppermute(x, "shot", swap_core), y)
                outs.append((lax.ppermute(send, "shot", swap_row), edge_keep))
            else:
                after, x, y = edge_step(half, scalars, *arrived, edge, gain, after)
                outs.append(exchange(x, y))
        previous = current
        current = after
        if not last:
            arrived_a, arrived_b = outs
    share = gather_sum(scalars, inner, *outs)
    return current[None], share


def solution(mesh):
    in_specs = (
        P("sub", None, None),
        P("shot", "sub", None, None),
        P("shot", "sub", None, None),
        P("shot", None, "sub", None, None),
        P("shot", None, "sub"),
        P("shot", "sub", None),
        P("shot", "sub"),
    )
    out_specs = (P("shot", "sub", None, None), P("sub", "shot", None))
    return jax.shard_map(shards, mesh=mesh, in_specs=in_specs, out_specs=out_specs, check_vma=False)
```

```python
import functools

import jax
import jax.numpy as jnp
import ml_dtypes
import numpy as np
from jax import lax
from jax.experimental import pallas as pl
from jax.experimental.pallas import tpu as pltpu
from jax.sharding import PartitionSpec as P

PML = 16
STEPS = 4
COEFFS = (-205.0 / 72.0, 8.0 / 5.0, -1.0 / 5.0, 8.0 / 315.0, -1.0 / 560.0)
COURANT = 0.09
DAMP_MAX = 0.3
RATIO = tuple(c / COEFFS[1] for c in COEFFS)
SLAB = 16
SIZE = 256
HALF = 128
CAP = 64
MIB = 1 << 20

bf16 = jnp.bfloat16
f32 = jnp.float32
VMEM = pl.BlockSpec(memory_space=pltpu.VMEM)
SMEM = pl.BlockSpec(memory_space=pltpu.SMEM)
ANY = pl.BlockSpec(memory_space=pl.ANY)


def params(mib, dims=1):
    return pltpu.CompilerParams(
        vmem_limit_bytes=mib * MIB, dimension_semantics=("arbitrary",) * dims if dims else None
    )


def pinned(x):
    return pltpu.with_memory_space_constraint(x, pltpu.VMEM)


def in_hbm(x):
    return pltpu.with_memory_space_constraint(x, pltpu.HBM)


def cost(flops, mib):
    return pl.CostEstimate(flops=int(flops), bytes_accessed=int(mib * MIB), transcendentals=0)


def profile(index, count):
    depth = jnp.maximum(jnp.maximum(PML - index, index - (count - 1 - PML)), 0.0) / PML
    return depth * depth


def band():
    m = np.zeros((SIZE, SIZE), np.float32)
    for k in range(1, 5):
        m += RATIO[k] * (np.eye(SIZE, k=k, dtype=np.float32) + np.eye(SIZE, k=-k, dtype=np.float32))
    return m.astype(ml_dtypes.bfloat16)


def route_body(slabs, target_ref, cell_ref, trace_ref, out_ref, pick):
    listed = target_ref.shape[1]
    slots = slabs * CAP
    target = target_ref[...]
    hot = (lax.broadcasted_iota(jnp.int32, (slabs, listed), 0) == target).astype(bf16)
    earlier = (
        lax.broadcasted_iota(jnp.int32, (listed, listed), 0)
        < lax.broadcasted_iota(jnp.int32, (listed, listed), 1)
    ).astype(bf16)
    before = jnp.dot(hot, earlier, preferred_element_type=f32)
    rank = jnp.sum(before * hot.astype(f32), axis=0, keepdims=True)
    place = target * CAP + rank.astype(jnp.int32)
    value = trace_ref[...]
    top = value.astype(bf16)
    rest = value - top.astype(f32)
    middle = rest.astype(bf16)
    last = (rest - middle.astype(f32)).astype(bf16)
    cell = cell_ref[...]
    pieces = jnp.concatenate(
        [(cell >> 12).astype(f32), ((cell >> 4) & 255).astype(f32), (cell & 15).astype(f32), jnp.zeros((1, listed), f32)],
        axis=0,
    ).astype(bf16)
    table = jnp.concatenate([top, middle, last, pieces], axis=0)
    out_ref[...] = jnp.zeros_like(out_ref)
    chunk = pick.shape[0]
    for start in range(0, slots, chunk):
        pick[...] = (
            lax.broadcasted_iota(jnp.int32, (chunk, listed), 0) + start == place
        ).astype(f32).astype(bf16)
        got = lax.dot_general(
            table, pick[...], (((1,), (1,)), ((), ())), preferred_element_type=f32
        )
        values = got[0:4] + got[4:8] + got[8:12]
        cells = got[12:13] * 4096.0 + got[13:14] * 16.0 + got[14:15]
        block = jnp.concatenate([values, jnp.broadcast_to(cells, (4, chunk))], axis=0)
        for j in range(chunk // CAP):
            out_ref[start // CAP + j, :, 0:CAP] = block[:, j * CAP : (j + 1) * CAP]


def route(target, cell, trace, slabs):
    return pl.pallas_call(
        functools.partial(route_body, slabs),
        out_shape=jax.ShapeDtypeStruct((slabs, 8, 128), f32),
        scratch_shapes=[pltpu.VMEM((256, target.shape[1]), bf16)],
        compiler_params=params(10, 0),
        cost_estimate=cost(1, 0),
        name="route",
    )(target, cell, trace)


def inject_body(value_ref, dense, cells_vmem, cell_ref, sem):
    cells_vmem[...] = value_ref[:, 4, :].astype(jnp.int32)
    copy = pltpu.make_async_copy(cells_vmem, cell_ref, sem)
    copy.start()
    zero = jnp.zeros((256, 128), f32)

    @pl.loop(0, dense.shape[0] // 256)
    def _(i):
        dense[pl.ds(pl.multiple_of(i * 256, 256), 256), :] = zero

    copy.wait()
    position = lax.broadcasted_iota(jnp.int32, (8, 128), 1) + 128 * (
        lax.broadcasted_iota(jnp.int32, (8, 128), 0) >> 2
    )
    batch = 2

    @pl.loop(0, value_ref.shape[0])
    def _(source):
        tile = value_ref[source]
        eight = jnp.concatenate([tile[0:4], tile[0:4]], axis=0)

        def some(first):
            cells = [cell_ref[source, first + j] for j in range(batch)]
            rows = [c >> 8 for c in cells]
            add = [
                jnp.where(position == (c & 255), eight[:, first + j : first + j + 1], 0.0)
                for j, c in enumerate(cells)
            ]
            at = [pl.ds(pl.multiple_of(r * 8, 8), 8) for r in rows]
            total = [dense[a, :] + u for a, u in zip(at, add)]
            for j in range(batch):
                for i in range(j):
                    same = (rows[i] == rows[j]).astype(f32)
                    total[j] = total[j] + same * add[i]
            for j in range(batch):
                dense[at[j], :] = total[j]

        for first in range(0, CAP, batch):
            some(first)


def source_of(dense, plane, start, step):
    base = (plane * SIZE + start) * 8 + step
    return jnp.concatenate([dense[pl.ds(base + half * 4, 8, stride=8), :] for half in range(2)], axis=1)


def inject(values):
    return pl.pallas_call(
        inject_body,
        out_shape=pltpu.VMEM((SLAB * SIZE * 8, 128), f32),
        in_specs=[VMEM],
        out_specs=VMEM,
        scratch_shapes=[
            pltpu.VMEM((values.shape[0], 128), jnp.int32),
            pltpu.SMEM((values.shape[0], 128), jnp.int32),
            pltpu.SemaphoreType.DMA,
        ],
        compiler_params=params(4, 0),
        cost_estimate=cost(1, 0),
        name="inject",
    )(values)


def side_of(group, parity):
    return (group + parity + 1) % 2


def first_edges_body(scalar_ref, source, *refs):
    sems = refs[4]
    copies = []
    for i in range(4):
        half, group = divmod(i, 2)
        start = 12 * side_of(group, scalar_ref[0])
        copies.append(
            pltpu.make_async_copy(
                source.at[pl.ds(start, 4), :, pl.ds(half * HALF, HALF)], refs[i], sems.at[i]
            )
        )
    for copy in copies:
        copy.start()
    for copy in copies:
        copy.wait()


def first_edges(current, scalars):
    return pl.pallas_call(
        first_edges_body,
        out_shape=[pltpu.VMEM((4, SIZE, HALF), f32)] * 4,
        in_specs=[SMEM, ANY],
        out_specs=[VMEM] * 4,
        scratch_shapes=[pltpu.SemaphoreType.DMA((4,))],
        compiler_params=params(4, 0),
        cost_estimate=cost(1, 0),
        name="first_edges",
    )(scalars, in_hbm(current))


def factor(speed, damp):
    inverse = 1.0 / (1.0 + damp)
    return inverse, (COURANT * COURANT) * (speed * speed) * inverse


def local_body(step, scalar_ref, damp_x_ref, q_hbm, p_hbm, v_ref, s_ref, damp_ref, band_ref, *rest):
    if step == 0:
        v_hbm = v_ref
        n_hbm, edge_ref, gain_ref, v_ref, *scratch = rest
    elif step == 1:
        n_hbm, edge_ref, gain_ref, *scratch = rest
    elif step == 2:
        accel_hbm, n_hbm, edge_ref, gain_ref, part, *scratch = rest
    else:
        accel_hbm, part, n_hbm, loc_ref, *scratch = rest
        (send_ref, keep_ref), scratch = scratch[:2], scratch[2:]
    high, low, mixed0, mixed1, q_ref, n_ref, load_sems, store_sems = scratch[:8]
    if step >= 2:
        accel, accel_sems = scratch[8:10]
    if step == 3:
        shared = scratch[10]
    p_ref = n_ref
    mixed = (mixed0, mixed1)
    group_size = 4
    groups = SLAB // group_size
    span = SIZE // group_size
    rows = 8 if step < 2 else 16
    core = scalar_ref[1]
    first = 0 if step == 2 else 2

    def planes(group):
        return pl.ds(group_size * group, group_size)

    def load(i, group):
        source, target = (q_hbm, q_ref) if i == 0 else (p_hbm, p_ref) if i == 1 else (v_hbm, v_ref)
        return pltpu.make_async_copy(
            source.at[planes(group)], target.at[planes(group)], load_sems.at[i, group]
        )

    def fetch(group):
        return pltpu.make_async_copy(
            accel_hbm.at[0, pl.ds(first, 2), planes(group)], accel.at[group], accel_sems.at[group]
        )

    def store(group):
        return pltpu.make_async_copy(
            n_ref.at[planes(group)], n_hbm.at[planes(group)], store_sems.at[group]
        )

    def others(group):
        out = [load(1, group)]
        if step == 0:
            out.append(load(2, group))
        if step >= 2:
            out.append(fetch(group))
        return out

    load(0, 0).start()
    for group in range(groups):
        if group + 1 < groups:
            load(0, group + 1).start()
        for copy in others(group):
            copy.start()
    load(0, 0).wait()

    def prepare(plane, into):
        here = q_ref[plane]
        top = here.astype(bf16)
        high[...] = top
        low[...] = (here - top.astype(f32)).astype(bf16)
        matrix = band_ref[...]
        into[...] = (
            jnp.dot(high[...], matrix, preferred_element_type=f32)
            + jnp.dot(low[...], matrix, preferred_element_type=f32)
            + jnp.dot(matrix, high[...], preferred_element_type=f32)
            + jnp.dot(matrix, low[...], preferred_element_type=f32)
        )

    def update(group, whole, offset):
        start = pl.multiple_of(whole + offset, rows)
        row = pl.ds(start, rows)
        lowest = group_size * group
        field = {x: q_ref[x, row, :] for x in range(max(0, lowest - 4), min(SLAB, lowest + group_size + 4))}
        damp = damp_ref[row, :]
        for plane in range(lowest, lowest + group_size):

            def rate(t):
                return accel[group, t, plane - lowest, row, :].astype(f32)

            around = mixed[group % 2][plane - lowest, row, :]
            for k in range(1, 5):
                both = [field[x] for x in (plane - k, plane + k) if 0 <= x < SLAB]
                term = both[0] if len(both) == 1 else both[0] + both[1]
                around = around + (term if k == 1 else RATIO[k] * term)
            now = field[plane]
            before = p_ref[plane, row, :]
            speed = v_ref[plane, row, :]
            inverse, gain = factor(speed, damp + damp_x_ref[plane])
            laplace = (3.0 * COEFFS[0]) * now + COEFFS[1] * around
            laplace = laplace + jnp.concatenate(
                [source_of(s_ref, plane, start + i * 8, step) for i in range(rows // 8)], axis=0
            )
            after = before + (2.0 * inverse) * (now - before) + gain * laplace
            n_ref[plane, row, :] = after
            if step == 2:
                part[plane, row, :] = before * rate(0) + now * rate(1)
            if step == 3:
                total = part[plane, row, :] + now * rate(0) + after * rate(1)
                grad = total * (2.0 / (speed * speed * speed))
                if plane < 4 or plane >= SLAB - 4:
                    loc_ref[plane if plane < 4 else plane - 8, row, :] = grad
                else:
                    shared[plane - lowest, pl.ds(start - whole, rows), :] = grad
            elif plane < 4 or plane >= SLAB - 4:
                edge_ref[plane if plane < 4 else plane - 8, row, :] = after
                gain_ref[plane if plane < 4 else plane - 8, row, :] = gain

    for plane in range(group_size):
        prepare(plane, mixed0.at[plane])
    for group in range(groups):
        if group + 1 < groups:
            load(0, group + 1).wait()
        for copy in others(group):
            copy.wait()

        @pl.loop(0, group_size)
        def _(j):
            if group + 1 < groups:
                prepare(group_size * (group + 1) + j, mixed[(group + 1) % 2].at[j])
            for i in range(span // rows):
                update(group, j * span, i * rows)
            if step == 3 and 0 < group < groups - 1:
                inner = pl.ds(group_size * (group - 1), group_size)

                @pl.when((j & 1) == core)
                def _():
                    keep_ref[inner, j >> 1] = shared[...]

                @pl.when((j & 1) != core)
                def _():
                    send_ref[inner, j >> 1] = shared[...]

        store(group).start()
    for group in range(groups):
        store(group).wait()


def local_step(step, scalars, damp_x, q, p, v, s, damp, accel, part=None):
    whole = (SLAB, SIZE, SIZE)
    in_specs = [SMEM, SMEM, ANY, ANY, VMEM if step else ANY] + [VMEM] * 3
    v = pinned(v) if step else in_hbm(v)
    operands = [scalars, damp_x, in_hbm(q), in_hbm(p), v, pinned(s), damp, jnp.asarray(band())]
    out_specs = [ANY]
    out_shape = [pltpu.HBM(whole, f32)]
    scratch = [
        pltpu.VMEM((SIZE, SIZE), bf16),
        pltpu.VMEM((SIZE, SIZE), bf16),
        pltpu.VMEM((4, SIZE, SIZE), f32),
        pltpu.VMEM((4, SIZE, SIZE), f32),
        pltpu.VMEM(whole, f32),
        pltpu.VMEM(whole, f32),
        pltpu.SemaphoreType.DMA((3, 4)),
        pltpu.SemaphoreType.DMA((4,)),
    ]
    if step >= 2:
        in_specs.append(ANY)
        operands.append(in_hbm(accel))
        scratch += [
            pltpu.VMEM((4, 2, 4, SIZE, SIZE), bf16),
            pltpu.SemaphoreType.DMA((4,)),
        ]
    if step < 3:
        out_specs += [VMEM] * 2
        out_shape += [jax.ShapeDtypeStruct((8, SIZE, SIZE), f32)] * 2
    if step in (0, 2):
        out_specs.append(VMEM)
        out_shape.append(pltpu.VMEM(whole, f32))
    if step == 3:
        in_specs.append(VMEM)
        operands.append(pinned(part))
        out_specs += [VMEM] * 3
        out_shape.append(jax.ShapeDtypeStruct((8, SIZE, SIZE), f32))
        out_shape += [jax.ShapeDtypeStruct((8, 2, 64, SIZE), f32)] * 2
        scratch.append(pltpu.VMEM((4, 64, SIZE), f32))
    return pl.pallas_call(
        functools.partial(local_body, step),
        out_shape=out_shape,
        in_specs=in_specs,
        out_specs=out_specs,
        scratch_shapes=scratch,
        compiler_params=params(24, 0),
        cost_estimate=cost(4e9, 20),
        name=f"local_step{step}",
    )(*operands)


def halo_weights(upper):
    return [
        [
            jnp.where(
                upper == 1,
                COEFFS[4 + m - j] if m <= j else 0.0,
                COEFFS[4 + j - m] if m >= j else 0.0,
            ).astype(f32)
            for m in range(4)
        ]
        for j in range(4)
    ]


def edge_body(half, scalar_ref, even_ref, odd_ref, edge_ref, gain_ref, _, n_hbm, e_ref, o_ref, sems):
    rows = 16
    lanes = slice(half * HALF, (half + 1) * HALF)
    copies = []
    for group in range(2):
        upper = side_of(group, scalar_ref[0])
        halo_ref, out_ref = ((even_ref, e_ref), (odd_ref, o_ref))[group]
        weights = halo_weights(upper)

        @pl.loop(0, SIZE // rows)
        def _(i):
            row = pl.ds(pl.multiple_of(i * rows, rows), rows)
            halo = [halo_ref[m, row, :] for m in range(4)]
            for j in range(4):
                across = weights[j][0] * halo[0]
                for m in range(1, 4):
                    across = across + weights[j][m] * halo[m]
                layer = upper * 4 + j
                out_ref[j, row, :] = edge_ref[layer, row, lanes] + gain_ref[layer, row, lanes] * across

        copies.append(
            pltpu.make_async_copy(
                out_ref, n_hbm.at[pl.ds(12 * upper, 4), :, pl.ds(half * HALF, HALF)], sems.at[group]
            )
        )
        copies[-1].start()
    for copy in copies:
        copy.wait()


def edge_step(half, scalars, even, odd, edge, gain, n):
    return pl.pallas_call(
        functools.partial(edge_body, half),
        out_shape=[pltpu.HBM((SLAB, SIZE, SIZE), f32)] + [jax.ShapeDtypeStruct((4, SIZE, HALF), f32)] * 2,
        in_specs=[SMEM] + [VMEM] * 4 + [ANY],
        out_specs=[ANY, VMEM, VMEM],
        scratch_shapes=[pltpu.SemaphoreType.DMA((2,))],
        input_output_aliases={5: 0},
        compiler_params=params(12, 0),
        cost_estimate=cost(1, 0),
        name=f"edge_step{half}",
    )(scalars, even, odd, edge, gain, in_hbm(n))


def last_edge_body(
    half,
    scalar_ref,
    damp_x_ref,
    even_ref,
    odd_ref,
    _,
    v_ref,
    damp_ref,
    a_hbm,
    loc_ref,
    n_hbm,
    send_ref,
    keep_ref,
    face,
    accel,
    grad,
    sems,
):
    core = scalar_ref[1]
    rows = 16
    lanes = slice(half * HALF, (half + 1) * HALF)

    def copy(group, which):
        at = (pl.ds(12 * side_of(group, scalar_ref[0]), 4), slice(None), pl.ds(half * HALF, HALF))
        there, here = n_hbm.at[at], face.at[group]
        if which == 0:
            return pltpu.make_async_copy(there, here, sems.at[group, 0])
        if which == 1:
            return pltpu.make_async_copy(a_hbm.at[(0, STEPS - 1, *at)], accel.at[group], sems.at[group, 1])
        return pltpu.make_async_copy(here, there, sems.at[group, 2])

    for group in range(2):
        copy(group, 0).start()
        copy(group, 1).start()
    for group in range(2):
        upper = side_of(group, scalar_ref[0])
        halo_ref = (even_ref, odd_ref)[group]
        weights = halo_weights(upper)
        copy(group, 0).wait()
        copy(group, 1).wait()

        @pl.loop(0, SIZE // rows)
        def _(i):
            row = pl.ds(pl.multiple_of(i * rows, rows), rows)
            halo = [halo_ref[m, row, :] for m in range(4)]
            damp = damp_ref[row, lanes]
            for j in range(4):
                layer = upper * 12 + j
                speed = v_ref[layer, row, lanes]
                _, gain = factor(speed, damp + damp_x_ref[layer])
                across = weights[j][0] * halo[0]
                for m in range(1, 4):
                    across = across + weights[j][m] * halo[m]
                extra = gain * across
                face[group, j, row, :] = face[group, j, row, :] + extra
                grad[j, row, :] = loc_ref[upper * 4 + j, row, lanes] + extra * accel[group, j, row, :].astype(
                    f32
                ) * (2.0 / (speed * speed * speed))

        copy(group, 2).start()
        for y in range(2):
            mine = pl.ds(pl.multiple_of(y * 128 + 64 * core, 64), 64)
            yours = pl.ds(pl.multiple_of(y * 128 + 64 * (1 - core), 64), 64)
            for j in range(4):
                keep_ref[group * 4 + j, y] = grad[j, mine, :]
                send_ref[group * 4 + j, y] = grad[j, yours, :]
    for group in range(2):
        copy(group, 2).wait()


def last_edge_step(half, scalars, damp_x, even, odd, n, v, damp, accel, loc):
    return pl.pallas_call(
        functools.partial(last_edge_body, half),
        out_shape=[pltpu.HBM((SLAB, SIZE, SIZE), f32)] + [jax.ShapeDtypeStruct((8, 2, 64, HALF), f32)] * 2,
        in_specs=[SMEM, SMEM, VMEM, VMEM, ANY, VMEM, VMEM, ANY, VMEM],
        out_specs=[ANY, VMEM, VMEM],
        scratch_shapes=[
            pltpu.VMEM((2, 4, SIZE, HALF), f32),
            pltpu.VMEM((2, 4, SIZE, HALF), bf16),
            pltpu.VMEM((4, SIZE, HALF), f32),
            pltpu.SemaphoreType.DMA((2, 3)),
        ],
        input_output_aliases={4: 0},
        compiler_params=params(12, 0),
        cost_estimate=cost(1, 0),
        name=f"last_edge_step{half}",
    )(scalars, damp_x, even, odd, in_hbm(n), pinned(v), damp, in_hbm(accel), loc)


def split_body(scalar_ref, got_ref, own_ref, send_ref, keep_ref):
    y = scalar_ref[2]
    send_ref[0] = got_ref[0, 1 - y] + own_ref[0, 1 - y]
    keep_ref[0] = got_ref[0, y] + own_ref[0, y]


def split_sum(scalars, got, own):
    layers, _, rows, width = got.shape
    step = pl.BlockSpec((1, 2, rows, width), lambda i, s: (i, 0, 0, 0))
    out = pl.BlockSpec((1, rows, width), lambda i, s: (i, 0, 0))
    return pl.pallas_call(
        split_body,
        out_shape=[jax.ShapeDtypeStruct((layers, rows, width), f32)] * 2,
        grid_spec=pltpu.PrefetchScalarGridSpec(
            num_scalar_prefetch=1, grid=(layers,), in_specs=[step, step], out_specs=[out, out]
        ),
        compiler_params=params(4),
        cost_estimate=cost(1, 0),
        name="split_sum",
    )(scalars, got, own)


def gather_body(scalar_ref, inner_a, inner_b, first_a, first_b, second_a, second_b, out_ref):
    out_ref[4 : SLAB - 4] = inner_a[...] + inner_b[...]
    for upper in range(2):
        group = (upper + scalar_ref[0] + 1) % 2
        face = pl.ds(group * 4, 4)
        layers = slice(12 * upper, 12 * upper + 4)
        out_ref[layers, :, 0:HALF] = first_a[face] + first_b[face]
        out_ref[layers, :, HALF:SIZE] = second_a[face] + second_b[face]


def gather_sum(scalars, inner, first, second):
    return pl.pallas_call(
        gather_body,
        out_shape=jax.ShapeDtypeStruct((SLAB, 64, SIZE), f32),
        in_specs=[SMEM] + [VMEM] * 6,
        out_specs=VMEM,
        compiler_params=params(8, 0),
        cost_estimate=cost(1, 0),
        name="gather_sum",
    )(scalars, *inner, *first, *second)


def shards(velocity, adjoint_now, adjoint_prev, forward_accel, traces, receiver_sub, receiver_cell):
    slabs = lax.axis_size("sub")
    slab = lax.axis_index("sub")
    shot = lax.axis_index("shot")
    pairs_even = [(i, i ^ 1) for i in range(slabs)]
    pairs_odd = [pair for a in range(1, slabs - 1, 2) for pair in ((a, a + 1), (a + 1, a))]
    shots = lax.axis_size("shot")
    swap_core = [(i, i ^ 1) for i in range(shots)]
    swap_row = [(i, i ^ 2) for i in range(shots)]
    scalars = jnp.stack([slab % 2, shot % 2, shot // 2]).astype(jnp.int32)
    start_x = (slab * SLAB).astype(f32)
    damp_x = DAMP_MAX * profile(start_x + jnp.arange(SLAB, dtype=f32), SLAB * slabs)
    line = profile(jnp.arange(SIZE, dtype=f32), SIZE)
    damp = DAMP_MAX * (line[:, None] + line[None, :])

    def exchange(even, odd):
        return lax.ppermute(even, "sub", pairs_even), lax.ppermute(odd, "sub", pairs_odd)

    even_a, odd_a, even_b, odd_b = first_edges(adjoint_now[0], scalars)
    arrived_a = exchange(even_a, odd_a)
    arrived_b = exchange(even_b, odd_b)

    listed = receiver_sub.shape[1]
    sent = route(
        receiver_sub.reshape(1, listed), receiver_cell.reshape(1, listed), traces[0], slabs
    )
    got = lax.all_to_all(sent, "sub", split_axis=0, concat_axis=0, tiled=True)

    source = inject(got)

    current = adjoint_now[0]
    previous = adjoint_prev[0]
    part = []
    for step in range(STEPS):
        last = step == STEPS - 1
        after, *extra = local_step(
            step, scalars, damp_x, current, previous, velocity, source, damp, forward_accel, *part
        )
        outs = []
        if last:
            loc, inner_send, inner_keep = extra
            arrived_a, arrived_b = lax.optimization_barrier((arrived_a, arrived_b))
        else:
            edge, gain, *part = extra
            if step == 0:
                (velocity,), part = part, []
        for half, arrived in enumerate((arrived_a, arrived_b)):
            if last:
                after, x, y = last_edge_step(
                    half, scalars, damp_x, *arrived, after, velocity, damp, forward_accel, loc
                )
                if half == 0:
                    inner_send, x = lax.optimization_barrier((inner_send, x))
                    send, inner_keep = split_sum(scalars, lax.ppermute(inner_send, "shot", swap_core), inner_keep)
                    send, after = lax.optimization_barrier((send, after))
                    inner = (lax.ppermute(send, "shot", swap_row), inner_keep)
                send, edge_keep = split_sum(scalars, lax.ppermute(x, "shot", swap_core), y)
                outs.append((lax.ppermute(send, "shot", swap_row), edge_keep))
            else:
                after, x, y = edge_step(half, scalars, *arrived, edge, gain, after)
                outs.append(exchange(x, y))
        previous = current
        current = after
        if not last:
            arrived_a, arrived_b = outs
    share = gather_sum(scalars, inner, *outs)
    return current[None], share


def solution(mesh):
    in_specs = (
        P("sub", None, None),
        P("shot", "sub", None, None),
        P("shot", "sub", None, None),
        P("shot", None, "sub", None, None),
        P("shot", None, "sub"),
        P("shot", "sub", None),
        P("shot", "sub"),
    )
    out_specs = (P("shot", "sub", None, None), P("sub", "shot", None))
    return jax.shard_map(shards, mesh=mesh, in_specs=in_specs, out_specs=out_specs, check_vma=False)
```

```python
import functools

import jax
import jax.numpy as jnp
import ml_dtypes
import numpy as np
from jax import lax
from jax.experimental import pallas as pl
from jax.experimental.pallas import tpu as pltpu
from jax.sharding import PartitionSpec as P

PML = 16
STEPS = 4
COEFFS = (-205.0 / 72.0, 8.0 / 5.0, -1.0 / 5.0, 8.0 / 315.0, -1.0 / 560.0)
COURANT = 0.09
DAMP_MAX = 0.3
RATIO = tuple(c / COEFFS[1] for c in COEFFS)
SLAB = 16
SIZE = 256
HALF = 128
CAP = 64
MIB = 1 << 20

bf16 = jnp.bfloat16
f32 = jnp.float32
VMEM = pl.BlockSpec(memory_space=pltpu.VMEM)
SMEM = pl.BlockSpec(memory_space=pltpu.SMEM)
ANY = pl.BlockSpec(memory_space=pl.ANY)


def params(mib, dims=1):
    return pltpu.CompilerParams(
        vmem_limit_bytes=mib * MIB, dimension_semantics=("arbitrary",) * dims if dims else None
    )


def pinned(x):
    return pltpu.with_memory_space_constraint(x, pltpu.VMEM)


def in_hbm(x):
    return pltpu.with_memory_space_constraint(x, pltpu.HBM)


def cost(flops, mib):
    return pl.CostEstimate(flops=int(flops), bytes_accessed=int(mib * MIB), transcendentals=0)


def profile(index, count):
    depth = jnp.maximum(jnp.maximum(PML - index, index - (count - 1 - PML)), 0.0) / PML
    return depth * depth


def band():
    m = np.zeros((SIZE, SIZE), np.float32)
    for k in range(1, 5):
        m += RATIO[k] * (np.eye(SIZE, k=k, dtype=np.float32) + np.eye(SIZE, k=-k, dtype=np.float32))
    return m.astype(ml_dtypes.bfloat16)


def route_body(slabs, target_hbm, cell_hbm, trace_hbm, out_ref, target_ref, cell_ref, trace_ref, pick, sems):
    loads = [
        pltpu.make_async_copy(source, here, sems.at[i])
        for i, (source, here) in enumerate(
            ((target_hbm, target_ref), (cell_hbm, cell_ref), (trace_hbm, trace_ref))
        )
    ]
    for load in loads:
        load.start()
    for load in loads:
        load.wait()
    listed = target_ref.shape[1]
    slots = slabs * CAP
    target = target_ref[...]
    hot = (lax.broadcasted_iota(jnp.int32, (slabs, listed), 0) == target).astype(bf16)
    earlier = (
        lax.broadcasted_iota(jnp.int32, (listed, listed), 0)
        < lax.broadcasted_iota(jnp.int32, (listed, listed), 1)
    ).astype(bf16)
    before = jnp.dot(hot, earlier, preferred_element_type=f32)
    rank = jnp.sum(before * hot.astype(f32), axis=0, keepdims=True)
    place = target * CAP + rank.astype(jnp.int32)
    value = trace_ref[...]
    top = value.astype(bf16)
    rest = value - top.astype(f32)
    middle = rest.astype(bf16)
    last = (rest - middle.astype(f32)).astype(bf16)
    cell = cell_ref[...]
    pieces = jnp.concatenate(
        [(cell >> 12).astype(f32), ((cell >> 4) & 255).astype(f32), (cell & 15).astype(f32), jnp.zeros((1, listed), f32)],
        axis=0,
    ).astype(bf16)
    table = jnp.concatenate([top, middle, last, pieces], axis=0)
    out_ref[...] = jnp.zeros_like(out_ref)
    chunk = pick.shape[0]
    for start in range(0, slots, chunk):
        pick[...] = (
            lax.broadcasted_iota(jnp.int32, (chunk, listed), 0) + start == place
        ).astype(f32).astype(bf16)
        got = lax.dot_general(
            table, pick[...], (((1,), (1,)), ((), ())), preferred_element_type=f32
        )
        values = got[0:4] + got[4:8] + got[8:12]
        cells = got[12:13] * 4096.0 + got[13:14] * 16.0 + got[14:15]
        block = jnp.concatenate([values, jnp.broadcast_to(cells, (4, chunk))], axis=0)
        for j in range(chunk // CAP):
            out_ref[start // CAP + j, :, 0:CAP] = block[:, j * CAP : (j + 1) * CAP]


def route(target, cell, trace, slabs):
    return pl.pallas_call(
        functools.partial(route_body, slabs),
        out_shape=jax.ShapeDtypeStruct((slabs, 8, 128), f32),
        in_specs=[ANY] * 3,
        out_specs=VMEM,
        scratch_shapes=[
            pltpu.VMEM(target.shape, jnp.int32),
            pltpu.VMEM(cell.shape, jnp.int32),
            pltpu.VMEM(trace.shape, f32),
            pltpu.VMEM((256, target.shape[1]), bf16),
            pltpu.SemaphoreType.DMA((3,)),
        ],
        compiler_params=params(10, 0),
        cost_estimate=cost(1, 0),
        name="route",
    )(in_hbm(target), in_hbm(cell), in_hbm(trace))


def inject_body(value_ref, dense, cells_vmem, cell_ref, sem):
    cells_vmem[...] = value_ref[:, 4, :].astype(jnp.int32)
    copy = pltpu.make_async_copy(cells_vmem, cell_ref, sem)
    copy.start()
    zero = jnp.zeros((256, 128), f32)

    @pl.loop(0, dense.shape[0] // 256)
    def _(i):
        dense[pl.ds(pl.multiple_of(i * 256, 256), 256), :] = zero

    copy.wait()
    position = lax.broadcasted_iota(jnp.int32, (8, 128), 1) + 128 * (
        lax.broadcasted_iota(jnp.int32, (8, 128), 0) >> 2
    )
    batch = 2

    @pl.loop(0, value_ref.shape[0])
    def _(source):
        tile = value_ref[source]
        eight = jnp.concatenate([tile[0:4], tile[0:4]], axis=0)

        def some(first):
            cells = [cell_ref[source, first + j] for j in range(batch)]
            rows = [c >> 8 for c in cells]
            add = [
                jnp.where(position == (c & 255), eight[:, first + j : first + j + 1], 0.0)
                for j, c in enumerate(cells)
            ]
            at = [pl.ds(pl.multiple_of(r * 8, 8), 8) for r in rows]
            total = [dense[a, :] + u for a, u in zip(at, add)]
            for j in range(batch):
                for i in range(j):
                    same = (rows[i] == rows[j]).astype(f32)
                    total[j] = total[j] + same * add[i]
            for j in range(batch):
                dense[at[j], :] = total[j]

        for first in range(0, CAP, batch):
            some(first)


def source_of(dense, plane, start, step):
    base = (plane * SIZE + start) * 8 + step
    return jnp.concatenate([dense[pl.ds(base + half * 4, 8, stride=8), :] for half in range(2)], axis=1)


def inject(values):
    return pl.pallas_call(
        inject_body,
        out_shape=pltpu.VMEM((SLAB * SIZE * 8, 128), f32),
        in_specs=[VMEM],
        out_specs=VMEM,
        scratch_shapes=[
            pltpu.VMEM((values.shape[0], 128), jnp.int32),
            pltpu.SMEM((values.shape[0], 128), jnp.int32),
            pltpu.SemaphoreType.DMA,
        ],
        compiler_params=params(4, 0),
        cost_estimate=cost(1, 0),
        name="inject",
    )(values)


def side_of(group, parity):
    return (group + parity + 1) % 2


def first_edges_body(scalar_ref, source, *refs):
    sems = refs[4]
    copies = []
    for i in range(4):
        half, group = divmod(i, 2)
        start = 12 * side_of(group, scalar_ref[0])
        for layer in range(4):
            copies.append(
                pltpu.make_async_copy(
                    source.at[start + layer, :, pl.ds(half * HALF, HALF)], refs[i].at[layer], sems.at[i, layer]
                )
            )
    for copy in copies:
        copy.start()
    for copy in copies:
        copy.wait()


def first_edges(current, scalars):
    return pl.pallas_call(
        first_edges_body,
        out_shape=[pltpu.VMEM((4, SIZE, HALF), f32)] * 4,
        in_specs=[SMEM, ANY],
        out_specs=[VMEM] * 4,
        scratch_shapes=[pltpu.SemaphoreType.DMA((4, 4))],
        compiler_params=params(4, 0),
        cost_estimate=cost(1, 0),
        name="first_edges",
    )(scalars, in_hbm(current))


def factor(speed, damp):
    inverse = 1.0 / (1.0 + damp)
    return inverse, (COURANT * COURANT) * (speed * speed) * inverse


def local_body(step, scalar_ref, damp_x_ref, q_hbm, p_hbm, v_ref, s_ref, damp_ref, band_ref, *rest):
    if step == 0:
        v_hbm = v_ref
        n_hbm, edge_ref, gain_ref, v_ref, *scratch = rest
    elif step == 1:
        n_hbm, edge_ref, gain_ref, *scratch = rest
    elif step == 2:
        accel_hbm, n_hbm, edge_ref, gain_ref, part, *scratch = rest
    else:
        accel_hbm, part, n_hbm, loc_ref, *scratch = rest
        (send_ref, keep_ref), scratch = scratch[:2], scratch[2:]
    high, low, mixed0, mixed1, q_ref, n_ref, load_sems, store_sems = scratch[:8]
    if step >= 2:
        accel, accel_sems = scratch[8:10]
    if step == 3:
        shared = scratch[10]
    p_ref = n_ref
    mixed = (mixed0, mixed1)
    group_size = 4
    groups = SLAB // group_size
    span = SIZE // group_size
    rows = 8 if step < 2 else 16
    core = scalar_ref[1]
    first = 0 if step == 2 else 2

    def planes(group):
        return pl.ds(group_size * group, group_size)

    def load(i, group):
        source, target = (q_hbm, q_ref) if i == 0 else (p_hbm, p_ref) if i == 1 else (v_hbm, v_ref)
        return pltpu.make_async_copy(
            source.at[planes(group)], target.at[planes(group)], load_sems.at[i, group]
        )

    def fetch(group):
        return pltpu.make_async_copy(
            accel_hbm.at[0, pl.ds(first, 2), planes(group)], accel.at[group], accel_sems.at[group]
        )

    def store(group):
        return pltpu.make_async_copy(
            n_ref.at[planes(group)], n_hbm.at[planes(group)], store_sems.at[group]
        )

    def store_rows(j):
        at = (planes(groups - 1), pl.ds(pl.multiple_of(j * span, span), span))
        return pltpu.make_async_copy(n_ref.at[at], n_hbm.at[at], store_sems.at[groups - 1 + j])

    def others(group):
        out = [load(1, group)]
        if step == 0:
            out.append(load(2, group))
        if step >= 2:
            out.append(fetch(group))
        return out

    load(0, 0).start()
    for group in range(groups):
        if group + 1 < groups:
            load(0, group + 1).start()
        for copy in others(group):
            copy.start()
    load(0, 0).wait()

    def prepare(plane, into):
        here = q_ref[plane]
        top = here.astype(bf16)
        high[...] = top
        low[...] = (here - top.astype(f32)).astype(bf16)
        matrix = band_ref[...]
        into[...] = (
            jnp.dot(high[...], matrix, preferred_element_type=f32)
            + jnp.dot(low[...], matrix, preferred_element_type=f32)
            + jnp.dot(matrix, high[...], preferred_element_type=f32)
            + jnp.dot(matrix, low[...], preferred_element_type=f32)
        )

    def update(group, whole, offset):
        start = pl.multiple_of(whole + offset, rows)
        row = pl.ds(start, rows)
        lowest = group_size * group
        field = {x: q_ref[x, row, :] for x in range(max(0, lowest - 4), min(SLAB, lowest + group_size + 4))}
        damp = damp_ref[row, :]
        for plane in range(lowest, lowest + group_size):

            def rate(t):
                return accel[group, t, plane - lowest, row, :].astype(f32)

            around = mixed[group % 2][plane - lowest, row, :]
            for k in range(1, 5):
                both = [field[x] for x in (plane - k, plane + k) if 0 <= x < SLAB]
                term = both[0] if len(both) == 1 else both[0] + both[1]
                around = around + (term if k == 1 else RATIO[k] * term)
            now = field[plane]
            before = p_ref[plane, row, :]
            speed = v_ref[plane, row, :]
            inverse, gain = factor(speed, damp + damp_x_ref[plane])
            laplace = (3.0 * COEFFS[0]) * now + COEFFS[1] * around
            laplace = laplace + jnp.concatenate(
                [source_of(s_ref, plane, start + i * 8, step) for i in range(rows // 8)], axis=0
            )
            after = before + (2.0 * inverse) * (now - before) + gain * laplace
            n_ref[plane, row, :] = after
            if step == 2:
                part[plane, row, :] = before * rate(0) + now * rate(1)
            if step == 3:
                total = part[plane, row, :] + now * rate(0) + after * rate(1)
                grad = total * (2.0 / (speed * speed * speed))
                if plane < 4 or plane >= SLAB - 4:
                    loc_ref[plane if plane < 4 else plane - 8, row, :] = grad
                else:
                    shared[plane - lowest, pl.ds(start - whole, rows), :] = grad
            elif plane < 4 or plane >= SLAB - 4:
                edge_ref[plane if plane < 4 else plane - 8, row, :] = after
                gain_ref[plane if plane < 4 else plane - 8, row, :] = gain

    for plane in range(group_size):
        prepare(plane, mixed0.at[plane])
    for group in range(groups):
        if group + 1 < groups:
            load(0, group + 1).wait()
        for copy in others(group):
            copy.wait()

        @pl.loop(0, group_size)
        def _(j):
            if group + 1 < groups:
                prepare(group_size * (group + 1) + j, mixed[(group + 1) % 2].at[j])
            for i in range(span // rows):
                update(group, j * span, i * rows)
            if step == 3 and 0 < group < groups - 1:
                inner = pl.ds(group_size * (group - 1), group_size)

                @pl.when((j & 1) == core)
                def _():
                    keep_ref[inner, j >> 1] = shared[...]

                @pl.when((j & 1) != core)
                def _():
                    send_ref[inner, j >> 1] = shared[...]

            if group == groups - 1:
                store_rows(j).start()

        if group < groups - 1:
            store(group).start()
    for group in range(groups - 1):
        store(group).wait()
    for j in range(group_size):
        store_rows(j).wait()


def local_step(step, scalars, damp_x, q, p, v, s, damp, accel, part=None):
    whole = (SLAB, SIZE, SIZE)
    in_specs = [SMEM, SMEM, ANY, ANY, VMEM if step else ANY] + [VMEM] * 3
    v = pinned(v) if step else in_hbm(v)
    operands = [scalars, damp_x, in_hbm(q), in_hbm(p), v, pinned(s), damp, jnp.asarray(band())]
    out_specs = [ANY]
    out_shape = [pltpu.HBM(whole, f32)]
    scratch = [
        pltpu.VMEM((SIZE, SIZE), bf16),
        pltpu.VMEM((SIZE, SIZE), bf16),
        pltpu.VMEM((4, SIZE, SIZE), f32),
        pltpu.VMEM((4, SIZE, SIZE), f32),
        pltpu.VMEM(whole, f32),
        pltpu.VMEM(whole, f32),
        pltpu.SemaphoreType.DMA((3, 4)),
        pltpu.SemaphoreType.DMA((7,)),
    ]
    if step >= 2:
        in_specs.append(ANY)
        operands.append(in_hbm(accel))
        scratch += [
            pltpu.VMEM((4, 2, 4, SIZE, SIZE), bf16),
            pltpu.SemaphoreType.DMA((4,)),
        ]
    if step < 3:
        out_specs += [VMEM] * 2
        out_shape += [jax.ShapeDtypeStruct((8, SIZE, SIZE), f32)] * 2
    if step in (0, 2):
        out_specs.append(VMEM)
        out_shape.append(pltpu.VMEM(whole, f32))
    if step == 3:
        in_specs.append(VMEM)
        operands.append(pinned(part))
        out_specs += [VMEM] * 3
        out_shape.append(jax.ShapeDtypeStruct((8, SIZE, SIZE), f32))
        out_shape += [jax.ShapeDtypeStruct((8, 2, 64, SIZE), f32)] * 2
        scratch.append(pltpu.VMEM((4, 64, SIZE), f32))
    return pl.pallas_call(
        functools.partial(local_body, step),
        out_shape=out_shape,
        in_specs=in_specs,
        out_specs=out_specs,
        scratch_shapes=scratch,
        compiler_params=params(24, 0),
        cost_estimate=cost(4e9, 20),
        name=f"local_step{step}",
    )(*operands)


def halo_weights(upper):
    return [
        [
            jnp.where(
                upper == 1,
                COEFFS[4 + m - j] if m <= j else 0.0,
                COEFFS[4 + j - m] if m >= j else 0.0,
            ).astype(f32)
            for m in range(4)
        ]
        for j in range(4)
    ]


def edge_body(half, scalar_ref, even_ref, odd_ref, edge_ref, gain_ref, _, n_hbm, e_ref, o_ref, sems):
    rows = 16
    lanes = slice(half * HALF, (half + 1) * HALF)
    copies = []
    for group in range(2):
        upper = side_of(group, scalar_ref[0])
        halo_ref, out_ref = ((even_ref, e_ref), (odd_ref, o_ref))[group]
        weights = halo_weights(upper)

        @pl.loop(0, SIZE // rows)
        def _(i):
            row = pl.ds(pl.multiple_of(i * rows, rows), rows)
            halo = [halo_ref[m, row, :] for m in range(4)]
            for j in range(4):
                across = weights[j][0] * halo[0]
                for m in range(1, 4):
                    across = across + weights[j][m] * halo[m]
                layer = upper * 4 + j
                out_ref[j, row, :] = edge_ref[layer, row, lanes] + gain_ref[layer, row, lanes] * across

        copies.append(
            pltpu.make_async_copy(
                out_ref, n_hbm.at[pl.ds(12 * upper, 4), :, pl.ds(half * HALF, HALF)], sems.at[group]
            )
        )
        copies[-1].start()
    for copy in copies:
        copy.wait()


def edge_step(half, scalars, even, odd, edge, gain, n):
    return pl.pallas_call(
        functools.partial(edge_body, half),
        out_shape=[pltpu.HBM((SLAB, SIZE, SIZE), f32)] + [jax.ShapeDtypeStruct((4, SIZE, HALF), f32)] * 2,
        in_specs=[SMEM] + [VMEM] * 4 + [ANY],
        out_specs=[ANY, VMEM, VMEM],
        scratch_shapes=[pltpu.SemaphoreType.DMA((2,))],
        input_output_aliases={5: 0},
        compiler_params=params(12, 0),
        cost_estimate=cost(1, 0),
        name=f"edge_step{half}",
    )(scalars, even, odd, edge, gain, in_hbm(n))


def last_edge_body(
    half,
    scalar_ref,
    damp_x_ref,
    even_ref,
    odd_ref,
    _,
    v_ref,
    damp_ref,
    a_hbm,
    loc_ref,
    n_hbm,
    send_ref,
    keep_ref,
    face,
    accel,
    grad,
    sems,
):
    core = scalar_ref[1]
    rows = 16
    lanes = slice(half * HALF, (half + 1) * HALF)

    def copy(group, which):
        at = (pl.ds(12 * side_of(group, scalar_ref[0]), 4), slice(None), pl.ds(half * HALF, HALF))
        there, here = n_hbm.at[at], face.at[group]
        if which == 0:
            return pltpu.make_async_copy(there, here, sems.at[group, 0])
        if which == 1:
            return pltpu.make_async_copy(a_hbm.at[(0, STEPS - 1, *at)], accel.at[group], sems.at[group, 1])
        return pltpu.make_async_copy(here, there, sems.at[group, 2])

    for group in range(2):
        copy(group, 0).start()
        copy(group, 1).start()
    for group in range(2):
        upper = side_of(group, scalar_ref[0])
        halo_ref = (even_ref, odd_ref)[group]
        weights = halo_weights(upper)
        copy(group, 0).wait()
        copy(group, 1).wait()

        @pl.loop(0, SIZE // rows)
        def _(i):
            row = pl.ds(pl.multiple_of(i * rows, rows), rows)
            halo = [halo_ref[m, row, :] for m in range(4)]
            damp = damp_ref[row, lanes]
            for j in range(4):
                layer = upper * 12 + j
                speed = v_ref[layer, row, lanes]
                _, gain = factor(speed, damp + damp_x_ref[layer])
                across = weights[j][0] * halo[0]
                for m in range(1, 4):
                    across = across + weights[j][m] * halo[m]
                extra = gain * across
                face[group, j, row, :] = face[group, j, row, :] + extra
                grad[j, row, :] = loc_ref[upper * 4 + j, row, lanes] + extra * accel[group, j, row, :].astype(
                    f32
                ) * (2.0 / (speed * speed * speed))

        copy(group, 2).start()
        for y in range(2):
            mine = pl.ds(pl.multiple_of(y * 128 + 64 * core, 64), 64)
            yours = pl.ds(pl.multiple_of(y * 128 + 64 * (1 - core), 64), 64)
            for j in range(4):
                keep_ref[group * 4 + j, y] = grad[j, mine, :]
                send_ref[group * 4 + j, y] = grad[j, yours, :]
    for group in range(2):
        copy(group, 2).wait()


def last_edge_step(half, scalars, damp_x, even, odd, n, v, damp, accel, loc):
    return pl.pallas_call(
        functools.partial(last_edge_body, half),
        out_shape=[pltpu.HBM((SLAB, SIZE, SIZE), f32)] + [jax.ShapeDtypeStruct((8, 2, 64, HALF), f32)] * 2,
        in_specs=[SMEM, SMEM, VMEM, VMEM, ANY, VMEM, VMEM, ANY, VMEM],
        out_specs=[ANY, VMEM, VMEM],
        scratch_shapes=[
            pltpu.VMEM((2, 4, SIZE, HALF), f32),
            pltpu.VMEM((2, 4, SIZE, HALF), bf16),
            pltpu.VMEM((4, SIZE, HALF), f32),
            pltpu.SemaphoreType.DMA((2, 3)),
        ],
        input_output_aliases={4: 0},
        compiler_params=params(12, 0),
        cost_estimate=cost(1, 0),
        name=f"last_edge_step{half}",
    )(scalars, damp_x, even, odd, in_hbm(n), pinned(v), damp, in_hbm(accel), loc)


def split_body(scalar_ref, got_ref, own_ref, send_ref, keep_ref):
    y = scalar_ref[2]
    send_ref[0] = got_ref[0, 1 - y] + own_ref[0, 1 - y]
    keep_ref[0] = got_ref[0, y] + own_ref[0, y]


def split_sum(scalars, got, own):
    layers, _, rows, width = got.shape
    step = pl.BlockSpec((1, 2, rows, width), lambda i, s: (i, 0, 0, 0))
    out = pl.BlockSpec((1, rows, width), lambda i, s: (i, 0, 0))
    return pl.pallas_call(
        split_body,
        out_shape=[jax.ShapeDtypeStruct((layers, rows, width), f32)] * 2,
        grid_spec=pltpu.PrefetchScalarGridSpec(
            num_scalar_prefetch=1, grid=(layers,), in_specs=[step, step], out_specs=[out, out]
        ),
        compiler_params=params(4),
        cost_estimate=cost(1, 0),
        name="split_sum",
    )(scalars, got, own)


def gather_body(scalar_ref, inner_a, inner_b, first_a, first_b, second_a, second_b, out_ref):
    out_ref[4 : SLAB - 4] = inner_a[...] + inner_b[...]
    for upper in range(2):
        group = (upper + scalar_ref[0] + 1) % 2
        face = pl.ds(group * 4, 4)
        layers = slice(12 * upper, 12 * upper + 4)
        out_ref[layers, :, 0:HALF] = first_a[face] + first_b[face]
        out_ref[layers, :, HALF:SIZE] = second_a[face] + second_b[face]


def gather_sum(scalars, inner, first, second):
    return pl.pallas_call(
        gather_body,
        out_shape=jax.ShapeDtypeStruct((SLAB, 64, SIZE), f32),
        in_specs=[SMEM] + [VMEM] * 6,
        out_specs=VMEM,
        compiler_params=params(8, 0),
        cost_estimate=cost(1, 0),
        name="gather_sum",
    )(scalars, *inner, *first, *second)


def shards(velocity, adjoint_now, adjoint_prev, forward_accel, traces, receiver_sub, receiver_cell):
    slabs = lax.axis_size("sub")
    slab = lax.axis_index("sub")
    shot = lax.axis_index("shot")
    pairs_even = [(i, i ^ 1) for i in range(slabs)]
    pairs_odd = [pair for a in range(1, slabs - 1, 2) for pair in ((a, a + 1), (a + 1, a))]
    shots = lax.axis_size("shot")
    swap_core = [(i, i ^ 1) for i in range(shots)]
    swap_row = [(i, i ^ 2) for i in range(shots)]
    scalars = jnp.stack([slab % 2, shot % 2, shot // 2]).astype(jnp.int32)
    start_x = (slab * SLAB).astype(f32)
    damp_x = DAMP_MAX * profile(start_x + jnp.arange(SLAB, dtype=f32), SLAB * slabs)
    line = profile(jnp.arange(SIZE, dtype=f32), SIZE)
    damp = DAMP_MAX * (line[:, None] + line[None, :])

    def exchange(even, odd):
        return lax.ppermute(even, "sub", pairs_even), lax.ppermute(odd, "sub", pairs_odd)

    even_a, odd_a, even_b, odd_b = first_edges(adjoint_now[0], scalars)
    arrived_a = exchange(even_a, odd_a)
    arrived_b = exchange(even_b, odd_b)

    listed = receiver_sub.shape[1]
    sent = route(
        receiver_sub.reshape(1, listed), receiver_cell.reshape(1, listed), traces[0], slabs
    )
    got = lax.all_to_all(sent, "sub", split_axis=0, concat_axis=0, tiled=True)

    source = inject(got)

    current = adjoint_now[0]
    previous = adjoint_prev[0]
    part = []
    for step in range(STEPS):
        last = step == STEPS - 1
        after, *extra = local_step(
            step, scalars, damp_x, current, previous, velocity, source, damp, forward_accel, *part
        )
        outs = []
        if last:
            loc, inner_send, inner_keep = extra
            arrived_a, arrived_b = lax.optimization_barrier((arrived_a, arrived_b))
        else:
            edge, gain, *part = extra
            if step == 0:
                (velocity,), part = part, []
        for half, arrived in enumerate((arrived_a, arrived_b)):
            if last:
                after, x, y = last_edge_step(
                    half, scalars, damp_x, *arrived, after, velocity, damp, forward_accel, loc
                )
                if half == 0:
                    inner_send, x = lax.optimization_barrier((inner_send, x))
                    send, inner_keep = split_sum(scalars, lax.ppermute(inner_send, "shot", swap_core), inner_keep)
                    send, after = lax.optimization_barrier((send, after))
                    inner = (lax.ppermute(send, "shot", swap_row), inner_keep)
                send, edge_keep = split_sum(scalars, lax.ppermute(x, "shot", swap_core), y)
                outs.append((lax.ppermute(send, "shot", swap_row), edge_keep))
            else:
                after, x, y = edge_step(half, scalars, *arrived, edge, gain, after)
                outs.append(exchange(x, y))
        previous = current
        current = after
        if not last:
            arrived_a, arrived_b = outs
    share = gather_sum(scalars, inner, *outs)
    return current[None], share


def solution(mesh):
    in_specs = (
        P("sub", None, None),
        P("shot", "sub", None, None),
        P("shot", "sub", None, None),
        P("shot", None, "sub", None, None),
        P("shot", None, "sub"),
        P("shot", "sub", None),
        P("shot", "sub"),
    )
    out_specs = (P("shot", "sub", None, None), P("sub", "shot", None))
    return jax.shard_map(shards, mesh=mesh, in_specs=in_specs, out_specs=out_specs, check_vma=False)
```
